512 devices in a mesh: mp: 16 (over y, z_hi, core), row: 8 (over z_lo), col: 4 (over x).
Axes of the slice: x: 4, y: 4, z: 16 (z_hi: 2, z_lo: 8; z = z_hi * 8 + z_lo), core: 2. Of those that a mesh axis runs over, the one named last changes fastest.
Arguments:
- activations: bfloat16 [16, 512, 4096], P('mp', None, 'row'), as said below
- weights: bfloat16 [16, 4096, 2048], P('mp', None, ('row', 'col')), may hold values from -6 to 6
Outputs:
- merged: float32 [4096, 2048], P(('row', 'col'), 'mp')
The draws below stay inside these ranges and needn't reach their ends.
Inputs may be any that keep to these rules, and one draw needn't show every extreme that they name: `activations`: calibration inputs of each checkpoint, features of differing scales.
All inputs are finite; a program needn't handle non-finite values.
Results may differ from the reference program's by a relative error of at most 0.0028.
Values may be sent and summed in bfloat16 or wider, within the bound.
A program may use at most 64 MiB of HBM per device.

```python
import jax
import jax.numpy as jnp
from jax import lax

D = 4096
E = 2048
TOK = 512
ITERS = 3
MODELS = 16


def draw_activations(key, part):
    key = jax.random.fold_in(key, 11)
    first, second = jax.random.split(key, 2)
    position = jnp.arange(D, dtype=jnp.float32) / D
    values = jax.random.truncated_normal(first, -6.0, 6.0, (MODELS, TOK, D), jnp.float32)
    jitter = jax.random.uniform(second, (MODELS, 1, D), jnp.float32, 0.0, 0.5)
    exponent = 0.48 * position + jitter
    scale = jnp.power(10.0, exponent)
    return (values * scale).astype(jnp.bfloat16)


def shard_levels(own_key, shape, cuts, low, top_value):
    gain = 1.0
    for dim, parts in cuts:
        draws = jax.random.uniform(jax.random.fold_in(jax.random.fold_in(own_key, 6), dim), (parts,), jnp.float32, low / len(cuts), top_value / len(cuts))
        gain = gain * jnp.repeat(jnp.exp(draws), shape[dim] // parts).reshape((-1,) + (1,) * (len(shape) - 1 - dim))
    return gain


def scatter_about(rng, shape, width, reach, cuts=(), held_as=jnp.bfloat16):
    loudness = shard_levels(rng, shape, cuts, -0.22, 0.18) if cuts else 1.0
    result = jax.random.normal(rng, shape, jnp.float32) * width * loudness
    return jnp.minimum(jnp.maximum(result, -reach), reach).astype(held_as)


def setup_inputs(seed: int = 0) -> dict:
    keys = jax.random.split(jax.random.key(seed), 3)
    return {
        "activations": draw_activations(jax.random.fold_in(keys[2], 71), 0),
        "weights": scatter_about(keys[1], (MODELS, D, E), 1.0, 6.0, ((0, 16), (2, 32))),
    }


def add_model(carry, pair):
    gram, rhs = carry
    inputs, weight = pair
    outputs = jnp.dot(inputs, weight, preferred_element_type=jnp.float32).astype(jnp.bfloat16)
    dims = (((0,), (0,)), ((), ()))
    gram = gram + lax.dot_general(inputs, inputs, dims, preferred_element_type=jnp.float32)
    rhs = rhs + lax.dot_general(inputs, outputs, dims, preferred_element_type=jnp.float32)
    return (gram, rhs), None


def reference(activations, weights):
    start = (jnp.zeros((D, D), jnp.float32), jnp.zeros((D, E), jnp.float32))
    (gram, rhs), _ = lax.scan(add_model, start, (activations, weights))
    merged = jnp.zeros((D, E), jnp.float32)
    residual = rhs
    direction = rhs
    norm_now = jnp.sum(residual * residual, axis=0)
    for step in range(ITERS):
        image = jnp.dot(gram, direction, precision=lax.Precision.HIGHEST, preferred_element_type=jnp.float32)
        alpha = norm_now / jnp.sum(direction * image, axis=0)
        merged = merged + alpha * direction
        residual = residual - alpha * image
        norm_next = jnp.sum(residual * residual, axis=0)
        direction = residual + (norm_next / norm_now) * direction
        norm_now = norm_next
    return merged
```

```python
import jax
import jax.numpy as jnp
from jax import lax
from jax.experimental import pallas as pl
from jax.experimental.pallas import tpu as pltpu
from jax.sharding import PartitionSpec as P

MESH = pl.DeviceIdType.MESH
F32 = jnp.float32
BF16 = jnp.bfloat16
NZ = 192
SH = 80
H0 = 48
COLS = 32


def fold(v):
    return v[:, :128] + v[:, 128:256] + v[:, 256:384] + v[:, 384:]


def kernel(
    a_hbm, w_hbm, out_ref,
    abuf, wbuf, yown, ycat, thl, ubuf, rbuf, img, res, dir1, dir2, dhl, curv, mblk, obuf,
    in_sem, zs, zr, xs, xr, fs, fr, ys, yr, us, ur, gs, gr, cs, cr, os, orr,
):
    mp = lax.axis_index("mp")
    zl = lax.axis_index("row")
    x = lax.axis_index("col")
    y = lax.div(mp, 4)
    zh = lax.rem(lax.div(mp, 2), 2)
    k = lax.rem(mp, 2)
    z = 8 * zh + zl
    me = 2 * y + k

    def dev(dx, dy, dz, dk):
        return (4 * dy + 2 * lax.div(dz, 8) + dk, lax.rem(dz, 8), dx)

    def remote(src, dst, send, recv, device):
        return pltpu.make_async_remote_copy(
            src_ref=src, dst_ref=dst, send_sem=send, recv_sem=recv, device_id=device, device_id_type=MESH
        )

    def at_z(d):
        return lax.rem(z + d + 16, 16)

    def at_x(d):
        return lax.rem(x + d + 4, 4)

    def member(b):
        return (4 * lax.div(b, 2) + 2 * zh + lax.rem(b, 2), zl, x)

    in_a = pltpu.make_async_copy(a_hbm.at[0], abuf.at[z], in_sem.at[0])
    in_w = pltpu.make_async_copy(w_hbm.at[0], wbuf, in_sem.at[1])
    in_a.start()
    in_w.start()

    to_y, to_z, to_k = lax.div(zl, 2), 8 * lax.rem(zl, 2) + me, lax.div(x, 2)
    from_y, from_k = lax.div(zl, 2), lax.rem(zl, 2)

    def out_self(dx):
        return (dx == x) & (to_y == y) & (to_z == z) & (to_k == k)

    def source(i, h):
        return 2 * k + i, from_y, 8 * h + 2 * y + zh, from_k

    barrier = pltpu.get_barrier_semaphore()

    def greet(device):
        pl.semaphore_signal(barrier, inc=1, device_id=device, device_id_type=MESH)

    greet(dev(x, y, at_z(1), k))
    greet(dev(x, y, at_z(-1), k))
    greet(dev(x, y, at_z(8), k))
    greet(dev(at_x(1), y, z, k))
    greet(dev(at_x(-1), y, z, k))

    @pl.loop(1, 8)
    def _(j):
        greet(member(lax.rem(me + j, 8)))

    selfs = jnp.int32(0)
    for i in range(2):
        for h in range(2):
            sx, sy, sz, sk = source(i, h)
            mine = (sx == x) & (sy == y) & (sz == z) & (sk == k)
            selfs = selfs + mine.astype(jnp.int32)

            @pl.when(jnp.logical_not(mine))
            def _():
                greet(dev(sx, sy, sz, sk))

    in_a.wait()
    in_w.wait()
    pl.semaphore_wait(barrier, 16 - selfs)

    def rows_of(part, shard):
        if part == 0:
            return pl.ds(0, NZ)
        return pl.ds(pl.multiple_of(NZ + SH * shard, 16), SH)

    def zcopy(d, part, s):
        sign = 1 - 2 * d
        ref = abuf.at[at_z(-sign * s), rows_of(part, x)]
        return remote(ref, ref, zs.at[d, part, s], zr.at[d, part, s], dev(x, y, at_z(sign), k))

    def zrecv(d, part, s):
        sign = 1 - 2 * d
        ref = abuf.at[at_z(-sign * (s + 1)), rows_of(part, x)]
        return remote(ref, ref, zs.at[d, part, s], zr.at[d, part, s], dev(x, y, at_z(sign), k))

    def xcopy(d, b):
        ref = abuf.at[b, rows_of(1, x)]
        return remote(ref, ref, xs.at[d, b], xr.at[d, b], dev(at_x(1 - 2 * d), y, z, k))

    def xrecv(d, b):
        ref = abuf.at[b, rows_of(1, at_x(2 * d - 1))]
        return remote(ref, ref, xs.at[d, b], xr.at[d, b], dev(at_x(1 - 2 * d), y, z, k))

    def half_rows(d, shard):
        if d == 0:
            return pl.ds(pl.multiple_of(NZ + SH * shard, 16), H0)
        return pl.ds(pl.multiple_of(NZ + SH * shard + H0, 16), SH - H0)

    def fcopy(d, b):
        ref = abuf.at[b, half_rows(d, at_x(2 * d - 1))]
        return remote(ref, ref, fs.at[d, b], fr.at[d, b], dev(at_x(1 - 2 * d), y, z, k))

    def frecv(d, b):
        ref = abuf.at[b, half_rows(d, at_x(2))]
        return remote(ref, ref, fs.at[d, b], fr.at[d, b], dev(at_x(1 - 2 * d), y, z, k))

    def pass_on(b):
        for d in range(2):
            xrecv(d, b).wait_recv()
            fcopy(d, b).start()

    for part in (1, 0):
        for d in range(2):
            zcopy(d, part, 0).start()

    @pl.loop(1, 9)
    def _(s):
        @pl.when(s <= 7)
        def _():
            zrecv(0, 1, s - 1).wait_recv()

            @pl.when(s <= 6)
            def _():
                zcopy(0, 1, s).start()

            for d in range(2):
                xcopy(d, at_z(-s)).start()

        zrecv(1, 1, s - 1).wait_recv()

        @pl.when(s <= 7)
        def _():
            zcopy(1, 1, s).start()

        for d in range(2):
            xcopy(d, at_z(s)).start()

        zrecv(0, 0, s - 1).wait_recv()

        @pl.when(s <= 7)
        def _():
            zcopy(0, 0, s).start()
            zrecv(1, 0, s - 1).wait_recv()

            @pl.when(s <= 6)
            def _():
                zcopy(1, 0, s).start()

        @pl.when(s >= 2)
        def _():
            pass_on(at_z(1 - s))
            pass_on(at_z(s - 1))

    pass_on(at_z(8))

    @pl.loop(1, 16)
    def _(j):
        for d in range(2):
            frecv(d, at_z(j)).wait_recv()
            xcopy(d, at_z(j)).wait_send()
            fcopy(d, at_z(j)).wait_send()

    @pl.loop(0, 8)
    def _(s):
        zcopy(0, 0, s).wait_send()
        zcopy(1, 1, s).wait_send()

        @pl.when(s <= 6)
        def _():
            zcopy(0, 1, s).wait_send()
            zcopy(1, 0, s).wait_send()

    def project(b, acc):
        w = wbuf[pl.ds(pl.multiple_of(512 * b, 512), 512), :]
        return acc + lax.dot_general(
            w, abuf[8 * zh + b], (((0,), (1,)), ((), ())), preferred_element_type=F32
        )

    yown[...] = lax.fori_loop(0, 8, project, jnp.zeros((2 * COLS, 512), F32)).astype(BF16)
    away = yown.at[pl.ds(pl.multiple_of(COLS * (1 - zh), COLS), COLS)]
    ycopy = remote(away, ycat.at[zh], ys, yr, dev(x, y, at_z(8), k))
    ycopy.start()
    ycat[zh] = yown[pl.ds(pl.multiple_of(COLS * zh, COLS), COLS)]
    remote(away, ycat.at[1 - zh], ys, yr, dev(x, y, at_z(8), k)).wait_recv()
    ycopy.wait_send()

    def all_reduce(rnd, block):
        def part(b):
            return remote(ubuf.at[b], rbuf.at[rnd, me], us.at[rnd, b], ur.at[rnd, me], member(b))

        def part_from(b):
            return remote(ubuf.at[b], rbuf.at[rnd, b], us.at[rnd, b], ur.at[rnd, b], member(b))

        def whole(b):
            return remote(img.at[rnd, me], img.at[rnd, me], gs.at[rnd, b], gr.at[rnd, me], member(b))

        def whole_from(b):
            return remote(img.at[rnd, b], img.at[rnd, b], gs.at[rnd, b], gr.at[rnd, b], member(b))

        @pl.loop(1, 8)
        def _(j):
            b = lax.rem(me + j, 8)
            ubuf[b] = block(b)
            part(b).start()

        rbuf[rnd, me] = block(me)

        @pl.loop(1, 8)
        def _(j):
            part_from(lax.rem(me + j, 8)).wait_recv()

        total = rbuf[rnd, 0]
        for b in range(1, 8):
            total = total + rbuf[rnd, b]
        img[rnd, me] = total

        @pl.loop(1, 8)
        def _(j):
            whole(lax.rem(me + j, 8)).start()

        @pl.loop(1, 8)
        def _(j):
            b = lax.rem(me + j, 8)
            whole_from(b).wait_recv()
            whole(b).wait_send()
            part(b).wait_send()

    def split(v):
        hi = v.astype(BF16)
        return hi, (v - hi.astype(F32)).astype(BF16)

    def set_direction(b, v):
        hi, lo = split(v)
        dhl[b, pl.ds(0, COLS)] = hi
        dhl[b, pl.ds(COLS, COLS)] = lo

    def tokens_times(h):
        def step(b, acc):
            return acc + lax.dot_general(
                dhl[b], abuf[8 * h + b], (((1,), (1,)), ((), ())), preferred_element_type=F32
            )

        both = lax.fori_loop(0, 8, step, jnp.zeros((2 * COLS, 512), F32))
        return both[:COLS] + both[COLS:]

    def rhs_block(b):
        return jnp.dot(ycat[0], abuf[b], preferred_element_type=F32) + jnp.dot(
            ycat[1], abuf[8 + b], preferred_element_type=F32
        )

    def image_block(b):
        both = jnp.dot(thl[0], abuf[b], preferred_element_type=F32) + jnp.dot(
            thl[1], abuf[8 + b], preferred_element_type=F32
        )
        return both[:COLS] + both[COLS:]

    def apply_gram(rnd):
        for h in range(2):
            hi, lo = split(tokens_times(h))
            thl[h, pl.ds(0, COLS)] = hi
            thl[h, pl.ds(COLS, COLS)] = lo
        all_reduce(rnd, image_block)

    def column_sum(term):
        acc = jnp.zeros((COLS, 128), F32)
        for b in range(8):
            acc = acc + fold(term(b))
        return jnp.sum(acc, axis=1, keepdims=True)

    all_reduce(0, rhs_block)
    norm = column_sum(lambda b: img[0, b] * img[0, b])
    for b in range(8):
        set_direction(b, img[0, b])
    apply_gram(1)
    alpha0 = norm / column_sum(lambda b: img[0, b] * img[1, b])
    for b in range(8):
        res[b] = img[0, b] - alpha0 * img[1, b]
    norm1 = column_sum(lambda b: res[b] * res[b])
    beta = norm1 / norm
    for b in range(8):
        dir1[b] = res[b] + beta * img[0, b]
        set_direction(b, dir1[b])
    apply_gram(2)
    alpha1 = norm1 / column_sum(lambda b: dir1[b] * img[2, b])
    for b in range(8):
        res[b] = res[b] - alpha1 * img[2, b]
    norm2 = column_sum(lambda b: res[b] * res[b])
    beta = norm2 / norm1
    for b in range(8):
        dir2[b] = res[b] + beta * dir1[b]
        set_direction(b, dir2[b])
    curvature = jnp.zeros((COLS, 128), F32)
    for h in range(2):
        image = tokens_times(h)
        curvature = curvature + fold(image * image)
    curv[me] = curvature

    def ccopy(b):
        return remote(curv.at[me], curv.at[me], cs.at[b], cr.at[me], member(b))

    def crecv(b):
        return remote(curv.at[b], curv.at[b], cs.at[b], cr.at[b], member(b))

    @pl.loop(1, 8)
    def _(j):
        ccopy(lax.rem(me + j, 8)).start()

    @pl.loop(1, 8)
    def _(j):
        b = lax.rem(me + j, 8)
        crecv(b).wait_recv()
        ccopy(b).wait_send()

    total = curv[0]
    for b in range(1, 8):
        total = total + curv[b]
    alpha2 = norm2 / jnp.sum(total, axis=1, keepdims=True)
    merged = alpha0 * img[0, me] + alpha1 * dir1[me] + alpha2 * dir2[me]

    slot = 2 * lax.rem(x, 2) + zh
    for dx in range(4):
        mblk[dx] = merged[:, 128 * dx : 128 * (dx + 1)]

    def ocopy(dx):
        return remote(mblk.at[dx], obuf.at[slot], os.at[dx], orr.at[slot], dev(dx, to_y, to_z, to_k))

    for dx in range(4):

        @pl.when(jnp.logical_not(out_self(dx)))
        def _():
            ocopy(dx).start()

        @pl.when(out_self(dx))
        def _():
            obuf[slot] = mblk[dx]

    for i in range(2):
        for h in range(2):
            sx, sy, sz, sk = source(i, h)
            mine = (sx == x) & (sy == y) & (sz == z) & (sk == k)

            @pl.when(jnp.logical_not(mine))
            def _():
                q = 2 * i + h
                remote(mblk.at[0], obuf.at[q], os.at[0], orr.at[q], dev(sx, sy, sz, sk)).wait_recv()

    for dx in range(4):

        @pl.when(jnp.logical_not(out_self(dx)))
        def _():
            ocopy(dx).wait_send()

    for q in range(4):
        out_ref[:, COLS * q : COLS * (q + 1)] = obuf[q].T


def local(activations, weights):
    dma = pltpu.SemaphoreType.DMA
    vmem = pltpu.VMEM
    return pl.pallas_call(
        kernel,
        out_shape=jax.ShapeDtypeStruct((128, 128), F32),
        in_specs=[pl.BlockSpec(memory_space=pl.ANY)] * 2,
        out_specs=pl.BlockSpec(memory_space=pltpu.VMEM),
        scratch_shapes=[
            vmem((16, 512, 512), BF16),
            vmem((4096, 64), BF16),
            vmem((2 * COLS, 512), BF16),
            vmem((2, COLS, 512), BF16),
            vmem((2, 2 * COLS, 512), BF16),
            vmem((8, COLS, 512), F32),
            vmem((3, 8, COLS, 512), F32),
            vmem((3, 8, COLS, 512), F32),
            vmem((8, COLS, 512), F32),
            vmem((8, COLS, 512), F32),
            vmem((8, COLS, 512), F32),
            vmem((8, 2 * COLS, 512), BF16),
            vmem((8, COLS, 128), F32),
            vmem((4, COLS, 128), F32),
            vmem((4, COLS, 128), F32),
            dma((2,)),
            dma((2, 2, 8)),
            dma((2, 2, 8)),
            dma((2, 16)),
            dma((2, 16)),
            dma((2, 16)),
            dma((2, 16)),
            dma,
            dma,
            dma((3, 8)),
            dma((3, 8)),
            dma((3, 8)),
            dma((3, 8)),
            dma((8,)),
            dma((8,)),
            dma((4,)),
            dma((4,)),
        ],
        compiler_params=pltpu.CompilerParams(
            collective_id=0, has_side_effects=True, vmem_limit_bytes=48 * 1024 * 1024
        ),
    )(activations, weights)


def solution(mesh):
    in_specs = (P("mp", None, "row"), P("mp", None, ("row", "col")))
    out_specs = P(("row", "col"), "mp")
    return jax.shard_map(local, mesh=mesh, in_specs=in_specs, out_specs=out_specs, check_vma=False)
```

```python
import jax
import jax.numpy as jnp
from jax import lax
from jax.experimental import pallas as pl
from jax.experimental.pallas import tpu as pltpu
from jax.sharding import PartitionSpec as P

MESH = pl.DeviceIdType.MESH
F32 = jnp.float32
BF16 = jnp.bfloat16
NZ = 96
SH = 80
COLS = 32


def fold(v):
    return v[:, :128] + v[:, 128:256] + v[:, 256:384] + v[:, 384:]


def total_of(v):
    return jnp.sum(v, axis=1, keepdims=True)


def kernel(
    a_hbm, w_hbm, out_ref,
    abuf, wbuf, yacc, yown, ycat, thl, ubuf, cbuf, rbuf, img, res, dir1, vacc, tok, curv, mblk, obuf,
    in_sem, zs, zr, xs, xr, fs, fr, ys, yr, cs, cr, us, ur, gs, gr, hs, hr, ks, kr, os, orr,
):
    mp = lax.axis_index("mp")
    zl = lax.axis_index("row")
    x = lax.axis_index("col")
    y = lax.div(mp, 4)
    zh = lax.rem(lax.div(mp, 2), 2)
    k = lax.rem(mp, 2)
    z = 8 * zh + zl
    me = 2 * y + k

    def dev(dx, dy, dz, dk):
        return (4 * dy + 2 * lax.div(dz, 8) + dk, lax.rem(dz, 8), dx)

    def remote(src, dst, send, recv, device):
        return pltpu.make_async_remote_copy(
            src_ref=src, dst_ref=dst, send_sem=send, recv_sem=recv, device_id=device, device_id_type=MESH
        )

    def at_z(d):
        return lax.rem(z + d + 16, 16)

    def at_x(d):
        return lax.rem(x + d + 4, 4)

    def at_y(d):
        return lax.rem(y + d, 4)

    def member(b):
        return (4 * lax.div(b, 2) + 2 * zh + lax.rem(b, 2), zl, x)

    in_a = pltpu.make_async_copy(a_hbm.at[0], abuf.at[z], in_sem.at[0])
    in_w = pltpu.make_async_copy(w_hbm.at[0], wbuf, in_sem.at[1])
    in_a.start()
    in_w.start()

    barrier = pltpu.get_barrier_semaphore()

    def greet(device):
        pl.semaphore_signal(barrier, inc=1, device_id=device, device_id_type=MESH)

    greet(dev(x, y, at_z(1), k))
    greet(dev(x, y, at_z(-1), k))
    greet(dev(at_x(1), y, z, k))
    greet(dev(at_x(-1), y, z, k))

    @pl.loop(1, 8)
    def _(j):
        greet(member(lax.rem(me + j, 8)))

    in_a.wait()
    pl.semaphore_wait(barrier, 11)

    def rows_of(part, shard):
        if part < 2:
            return pl.ds(NZ * part, NZ)
        return pl.ds(pl.multiple_of(2 * NZ + SH * shard, 16), SH)

    def steps(d, part):
        return 8 if (part < 2) == (d == 0) else 7

    def zlink(d, part, s, distance):
        sign = 1 - 2 * d
        ref = abuf.at[at_z(-sign * distance), rows_of(part, x)]
        return remote(ref, ref, zs.at[d, part, s], zr.at[d, part, s], dev(x, y, at_z(sign), k))

    def zcopy(d, part, s):
        return zlink(d, part, s, s)

    def zrecv(d, part, s):
        return zlink(d, part, s, s + 1)

    def xcopy(d, b):
        ref = abuf.at[b, rows_of(2, x)]
        return remote(ref, ref, xs.at[d, b], xr.at[d, b], dev(at_x(1 - 2 * d), y, z, k))

    def xrecv(d, b):
        ref = abuf.at[b, rows_of(2, at_x(2 * d - 1))]
        return remote(ref, ref, xs.at[d, b], xr.at[d, b], dev(at_x(1 - 2 * d), y, z, k))

    def fcopy(d, b):
        ref = abuf.at[b, rows_of(2, at_x(2 * d - 1)), pl.ds(256 * d, 256)]
        return remote(ref, ref, fs.at[d, b], fr.at[d, b], dev(at_x(1 - 2 * d), y, z, k))

    def frecv(d, b):
        ref = abuf.at[b, rows_of(2, at_x(2)), pl.ds(256 * d, 256)]
        return remote(ref, ref, fs.at[d, b], fr.at[d, b], dev(at_x(1 - 2 * d), y, z, k))

    def pass_on(b):
        for d in range(2):
            xrecv(d, b).wait_recv()
            fcopy(d, b).start()

    def project(b):
        w = wbuf[:, pl.ds(pl.multiple_of(512 * lax.rem(b, 8), 512), 512)]
        yacc[...] += lax.dot_general(w, abuf[b], (((1,), (1,)), ((), ())), preferred_element_type=F32)

    def settle(b):
        for d in range(2):
            frecv(d, b).wait_recv()

        @pl.when(lax.div(b, 8) == zh)
        def _():
            project(b)

    for part in (2, 0, 1):
        for d in range(2):
            zcopy(d, part, 0).start()
    in_w.wait()
    yacc[...] = jnp.zeros_like(yacc)
    project(z)

    @pl.loop(1, 9)
    def _(s):
        def forward(d, part):
            n = steps(d, part)

            def body():
                zrecv(d, part, s - 1).wait_recv()

                def go():
                    zcopy(d, part, s).start()

                pl.when(s <= n - 1)(go)
                if part == 2:
                    for e in range(2):
                        xcopy(e, at_z((2 * d - 1) * s)).start()

            if n == 8:
                body()
            else:
                pl.when(s <= 7)(body)

        for part in (2, 0, 1):
            for d in range(2):
                forward(d, part)

        @pl.when(s >= 2)
        def _():
            pass_on(at_z(1 - s))
            pass_on(at_z(s - 1))

        @pl.when(s >= 3)
        def _():
            settle(at_z(2 - s))
            settle(at_z(s - 2))

    pass_on(at_z(8))
    settle(at_z(-7))
    settle(at_z(7))
    yown[...] = yacc[...].astype(BF16)
    away = yown.at[pl.ds(pl.multiple_of(COLS * (1 - zh), COLS), COLS)]
    partner = dev(x, y, at_z(8), k)
    ycopy = remote(away, ycat.at[zh], ys, yr, partner)
    ycopy.start()
    ycat[zh] = yown[pl.ds(pl.multiple_of(COLS * zh, COLS), COLS)]

    @pl.loop(0, 8)
    def _(b):
        ubuf[b] = jnp.dot(ycat[zh], abuf[8 * zh + b], preferred_element_type=F32)

    settle(at_z(8))

    @pl.loop(1, 16)
    def _(j):
        for d in range(2):
            xcopy(d, at_z(j)).wait_send()
            fcopy(d, at_z(j)).wait_send()

    for d in range(2):
        for part in range(3):

            @pl.loop(0, steps(d, part))
            def _(s):
                zcopy(d, part, s).wait_send()

    remote(away, ycat.at[1 - zh], ys, yr, partner).wait_recv()
    ycopy.wait_send()

    sibling = dev(x, y, z, 1 - k)

    def all_reduce(rnd, block, arrive):
        def core_part(o):
            q = at_y(o)
            return remote(ubuf.at[2 * q + 1 - k], cbuf.at[rnd, q], cs.at[rnd, q], cr.at[rnd, q], sibling)

        def ring_part(o):
            q = at_y(o)
            return remote(ubuf.at[2 * q + k], rbuf.at[rnd, y], us.at[rnd, q], ur.at[rnd, y], dev(x, q, z, k))

        def ring_part_from(o):
            q = at_y(o)
            return remote(ubuf.at[2 * q + k], rbuf.at[rnd, q], us.at[rnd, q], ur.at[rnd, q], dev(x, q, z, k))

        def ring_whole(o):
            q = at_y(o)
            ref = img.at[rnd, me]
            return remote(ref, ref, gs.at[rnd, q], gr.at[rnd, y], dev(x, q, z, k))

        def ring_whole_from(o):
            q = at_y(o)
            ref = img.at[rnd, 2 * q + k]
            return remote(ref, ref, gs.at[rnd, q], gr.at[rnd, q], dev(x, q, z, k))

        def core_whole(o):
            q = at_y(o)
            ref = img.at[rnd, 2 * q + k]
            return remote(ref, ref, hs.at[rnd, q], hr.at[rnd, q], sibling)

        def core_whole_from(o):
            q = at_y(o)
            ref = img.at[rnd, 2 * q + 1 - k]
            return remote(ref, ref, hs.at[rnd, q], hr.at[rnd, q], sibling)

        def give(o):
            b = 2 * at_y(o) + 1 - k
            ubuf[b] = block(b)
            core_part(o).start()

        def keep(o):
            q = at_y(o)
            b = 2 * q + k
            mine = block(b)
            remote(ubuf.at[b], cbuf.at[rnd, q], cs.at[rnd, q], cr.at[rnd, q], sibling).wait_recv()
            if o:
                ubuf[b] = mine + cbuf[rnd, q]
                ring_part(o).start()
            else:
                img[rnd, me] = mine + cbuf[rnd, q]

        give(2)
        give(1)
        keep(2)
        give(3)
        keep(1)
        give(0)
        keep(3)
        keep(0)
        for o in (1, 3, 2):
            ring_part_from(o).wait_recv()
        img[rnd, me] += rbuf[rnd, at_y(1)] + rbuf[rnd, at_y(3)] + rbuf[rnd, at_y(2)]
        for o in (2, 1, 3):
            ring_whole(o).start()
        core_whole(0).start()
        arrive(me)
        core_whole_from(0).wait_recv()
        arrive(2 * y + 1 - k)
        for o in (1, 3, 2):
            ring_whole_from(o).wait_recv()
            core_whole(o).start()
            arrive(2 * at_y(o) + k)
        for o in (1, 3, 2):
            core_whole_from(o).wait_recv()
            arrive(2 * at_y(o) + 1 - k)
        for o in range(4):
            core_part(o).wait_send()
            core_whole(o).wait_send()
            if o:
                ring_part(o).wait_send()
                ring_whole(o).wait_send()

    def split(v):
        hi = v.astype(BF16)
        return hi, (v - hi.astype(F32)).astype(BF16)

    def tokens_times(v, b):
        both = jnp.concatenate(split(v), axis=0)
        for h in range(2):
            vacc[h] += lax.dot_general(
                both, abuf[8 * h + b], (((1,), (1,)), ((), ())), preferred_element_type=F32
            )

    def products(h):
        return vacc[h, :COLS] + vacc[h, COLS:]

    def set_tokens(h, v):
        hi, lo = split(v)
        thl[h, pl.ds(0, COLS)] = hi
        thl[h, pl.ds(COLS, COLS)] = lo

    def rhs_block(b):
        return ubuf[b] + jnp.dot(ycat[1 - zh], abuf[8 * (1 - zh) + b], preferred_element_type=F32)

    def image_block(b):
        both = jnp.dot(thl[0], abuf[b], preferred_element_type=F32) + jnp.dot(
            thl[1], abuf[8 + b], preferred_element_type=F32
        )
        return both[:COLS] + both[COLS:]

    def column_sum(term):
        acc = jnp.zeros((COLS, 128), F32)
        for b in range(8):
            acc = acc + fold(term(b))
        return total_of(acc)

    def arrived(rnd):
        def go(b):
            tokens_times(img[rnd, b], b)

        return go

    vacc[...] = jnp.zeros_like(vacc)
    all_reduce(0, rhs_block, arrived(0))
    for h in range(2):
        t = products(h)
        set_tokens(h, t)
        tok[0, h] = t
        tok[1, h] = t
    vacc[...] = jnp.zeros_like(vacc)
    all_reduce(1, image_block, arrived(1))
    norm = column_sum(lambda b: img[0, b] * img[0, b])
    alpha0 = norm / column_sum(lambda b: img[0, b] * img[1, b])
    for b in range(8):
        res[b] = img[0, b] - alpha0 * img[1, b]
    norm1 = column_sum(lambda b: res[b] * res[b])
    beta = norm1 / norm
    for h in range(2):
        t = tok[1, h] - alpha0 * products(h)
        tok[1, h] = t
        t = t + beta * tok[0, h]
        tok[0, h] = t
        set_tokens(h, t)
    for b in range(8):
        dir1[b] = res[b] + beta * img[0, b]
    vacc[...] = jnp.zeros_like(vacc)
    all_reduce(2, image_block, arrived(2))
    alpha1 = norm1 / column_sum(lambda b: dir1[b] * img[2, b])
    for b in range(8):
        res[b] = res[b] - alpha1 * img[2, b]
    norm2 = column_sum(lambda b: res[b] * res[b])
    beta = norm2 / norm1
    square = jnp.zeros((COLS, 128), F32)
    for h in range(2):
        t = tok[1, h] - alpha1 * products(h) + beta * tok[0, h]
        square = square + fold(t * t)
    curv[me] = square

    def kcopy(b):
        return remote(curv.at[me], curv.at[me], ks.at[b], kr.at[me], member(b))

    def krecv(b):
        return remote(curv.at[b], curv.at[b], ks.at[b], kr.at[b], member(b))

    @pl.loop(1, 8)
    def _(j):
        kcopy(lax.rem(me + j, 8)).start()

    known = alpha0 * img[0, me] + alpha1 * dir1[me]
    last = res[me] + beta * dir1[me]

    @pl.loop(1, 8)
    def _(j):
        b = lax.rem(me + j, 8)
        krecv(b).wait_recv()
        kcopy(b).wait_send()

    curvature = curv[0]
    for b in range(1, 8):
        curvature = curvature + curv[b]
    alpha2 = norm2 / total_of(curvature)
    merged = known + alpha2 * last

    to_y, to_z, to_k = lax.div(zl, 2), 8 * lax.rem(zl, 2) + me, lax.div(x, 2)
    from_y, from_k = lax.div(zl, 2), lax.rem(zl, 2)
    slot = 2 * lax.rem(x, 2) + zh

    def out_self(dx):
        return (dx == x) & (to_y == y) & (to_z == z) & (to_k == k)

    def ocopy(dx):
        return remote(mblk.at[dx], obuf.at[slot], os.at[dx], orr.at[slot], dev(dx, to_y, to_z, to_k))

    for dx in range(4):
        mblk[dx] = merged[:, 128 * dx : 128 * (dx + 1)]

        @pl.when(jnp.logical_not(out_self(dx)))
        def _():
            ocopy(dx).start()

        @pl.when(out_self(dx))
        def _():
            obuf[slot] = mblk[dx]

    for i in range(2):
        for h in range(2):
            q = 2 * i + h
            sx, sz = 2 * k + i, 8 * h + 2 * y + zh
            mine = (sx == x) & (from_y == y) & (sz == z) & (from_k == k)

            @pl.when(jnp.logical_not(mine))
            def _():
                remote(mblk.at[0], obuf.at[q], os.at[0], orr.at[q], dev(sx, from_y, sz, from_k)).wait_recv()

    for dx in range(4):

        @pl.when(jnp.logical_not(out_self(dx)))
        def _():
            ocopy(dx).wait_send()

    for q in range(4):
        out_ref[:, COLS * q : COLS * (q + 1)] = obuf[q].T


def local(activations, weights):
    dma = pltpu.SemaphoreType.DMA
    vmem = pltpu.VMEM
    return pl.pallas_call(
        kernel,
        out_shape=jax.ShapeDtypeStruct((128, 128), F32),
        in_specs=[pl.BlockSpec(memory_space=pl.ANY)] * 2,
        out_specs=pl.BlockSpec(memory_space=pltpu.VMEM),
        scratch_shapes=[
            vmem((16, 512, 512), BF16),
            vmem((2 * COLS, 4096), BF16),
            vmem((2 * COLS, 512), F32),
            vmem((2 * COLS, 512), BF16),
            vmem((2, COLS, 512), BF16),
            vmem((2, 2 * COLS, 512), BF16),
            vmem((8, COLS, 512), F32),
            vmem((3, 4, COLS, 512), F32),
            vmem((3, 4, COLS, 512), F32),
            vmem((3, 8, COLS, 512), F32),
            vmem((8, COLS, 512), F32),
            vmem((8, COLS, 512), F32),
            vmem((2, 2 * COLS, 512), F32),
            vmem((2, 2, COLS, 512), F32),
            vmem((8, COLS, 128), F32),
            vmem((4, COLS, 128), F32),
            vmem((4, COLS, 128), F32),
            dma((2,)),
            dma((2, 3, 8)),
            dma((2, 3, 8)),
            dma((2, 16)),
            dma((2, 16)),
            dma((2, 16)),
            dma((2, 16)),
            dma,
            dma,
            dma((3, 4)),
            dma((3, 4)),
            dma((3, 4)),
            dma((3, 4)),
            dma((3, 4)),
            dma((3, 4)),
            dma((3, 4)),
            dma((3, 4)),
            dma((8,)),
            dma((8,)),
            dma((4,)),
            dma((4,)),
        ],
        compiler_params=pltpu.CompilerParams(
            collective_id=0, has_side_effects=True, vmem_limit_bytes=62 * 1024 * 1024
        ),
    )(activations, jnp.swapaxes(weights, 1, 2))


def solution(mesh):
    in_specs = (P("mp", None, "row"), P("mp", None, ("row", "col")))
    out_specs = P(("row", "col"), "mp")
    return jax.shard_map(local, mesh=mesh, in_specs=in_specs, out_specs=out_specs, check_vma=False)
```

```python
import jax
import jax.numpy as jnp
from jax import lax
from jax.experimental import pallas as pl
from jax.experimental.pallas import tpu as pltpu
from jax.sharding import PartitionSpec as P

MESH = pl.DeviceIdType.MESH
F32 = jnp.float32
BF16 = jnp.bfloat16
NZ = (96, 80)
NP = len(NZ)
ZS = sum(NZ)
HALF = 176
COLS = 32


def fold(v):
    return v[:, :128] + v[:, 128:256] + v[:, 256:384] + v[:, 384:]


def total_of(v):
    return jnp.sum(v, axis=1, keepdims=True)


def kernel(
    a_hbm, w_hbm, out_ref,
    abuf, wbuf, yacc, yown, ycat, thl, ubuf, cbuf, rbuf, img, res, dir1, vacc, tok, dots, curv, mblk, obuf,
    in_sem, zs, zr, xs, xr, fs, fr, es, er, ys, yr, cs, cr, us, ur, gs, gr, hs, hr, ks, kr, os, orr,
):
    mp = lax.axis_index("mp")
    zl = lax.axis_index("row")
    x = lax.axis_index("col")
    y = lax.div(mp, 4)
    zh = lax.rem(lax.div(mp, 2), 2)
    k = lax.rem(mp, 2)
    z = 8 * zh + zl
    me = 2 * y + k

    def dev(dx, dy, dz, dk):
        return (4 * dy + 2 * lax.div(dz, 8) + dk, lax.rem(dz, 8), dx)

    def remote(src, dst, send, recv, device):
        return pltpu.make_async_remote_copy(
            src_ref=src, dst_ref=dst, send_sem=send, recv_sem=recv, device_id=device, device_id_type=MESH
        )

    def at_z(d):
        return lax.rem(z + d + 16, 16)

    def at_x(d):
        return lax.rem(x + d + 4, 4)

    def at_y(d):
        return lax.rem(y + d, 4)

    def member(b):
        return (4 * lax.div(b, 2) + 2 * zh + lax.rem(b, 2), zl, x)

    in_a = pltpu.make_async_copy(a_hbm.at[0], abuf.at[z], in_sem.at[0])
    in_w = pltpu.make_async_copy(w_hbm.at[0], wbuf, in_sem.at[1])
    in_a.start()
    in_w.start()

    barrier = pltpu.get_barrier_semaphore()

    def greet(device):
        pl.semaphore_signal(barrier, inc=1, device_id=device, device_id_type=MESH)

    greet(dev(x, y, at_z(1), k))
    greet(dev(x, y, at_z(-1), k))
    greet(dev(at_x(1), y, z, k))
    greet(dev(at_x(-1), y, z, k))

    @pl.loop(1, 8)
    def _(j):
        greet(member(lax.rem(me + j, 8)))

    in_a.wait()
    pl.semaphore_wait(barrier, 11)

    def piece(b, part, shard):
        if part < NP:
            return abuf.at[b, pl.ds(sum(NZ[:part]), NZ[part])]
        return abuf.at[b, pl.ds(ZS, 512 - ZS), pl.ds(pl.multiple_of(128 * shard, 128), 128)]

    def half_piece(b, d, shard):
        rows = pl.ds(ZS, HALF) if d == 0 else pl.ds(ZS + HALF, 512 - ZS - HALF)
        return abuf.at[b, rows, pl.ds(pl.multiple_of(128 * shard, 128), 128)]

    def steps(d, part):
        return 8 if (part < NP) == (d == 0) else 7

    def zlink(d, part, s, distance):
        sign = 1 - 2 * d
        ref = piece(at_z(-sign * distance), part, x)
        return remote(ref, ref, zs.at[d, part, s], zr.at[d, part, s], dev(x, y, at_z(sign), k))

    def zcopy(d, part, s):
        return zlink(d, part, s, s)

    def zrecv(d, part, s):
        return zlink(d, part, s, s + 1)

    def xcopy(d, b):
        ref = piece(b, NP, x)
        return remote(ref, ref, xs.at[d, b], xr.at[d, b], dev(at_x(1 - 2 * d), y, z, k))

    def xrecv(d, b):
        ref = piece(b, NP, at_x(2 * d - 1))
        return remote(ref, ref, xs.at[d, b], xr.at[d, b], dev(at_x(1 - 2 * d), y, z, k))

    def fcopy(d, b):
        ref = half_piece(b, d, at_x(2 * d - 1))
        return remote(ref, ref, fs.at[d, b], fr.at[d, b], dev(at_x(1 - 2 * d), y, z, k))

    def frecv(d, b):
        ref = half_piece(b, d, at_x(2))
        return remote(ref, ref, fs.at[d, b], fr.at[d, b], dev(at_x(1 - 2 * d), y, z, k))

    def finish(i, b):
        ref = piece(b, NP, at_x((1, -1, 2)[i]))
        return remote(ref, ref, es.at[i], er.at[i], dev(x, y, at_z(1 if i == 0 else -1), k))

    def pass_on(b):
        for d in range(2):
            xrecv(d, b).wait_recv()
            fcopy(d, b).start()

    def project(b):
        w = wbuf[:, pl.ds(pl.multiple_of(512 * lax.rem(b, 8), 512), 512)]
        yacc[...] += lax.dot_general(w, abuf[b], (((1,), (1,)), ((), ())), preferred_element_type=F32)

    def settle(b):
        for d in range(2):
            frecv(d, b).wait_recv()

        @pl.when(lax.div(b, 8) == zh)
        def _():
            project(b)

    for part in (NP, *range(NP)):
        for d in range(2):
            zcopy(d, part, 0).start()
    in_w.wait()
    yacc[...] = jnp.zeros_like(yacc)
    project(z)

    @pl.loop(1, 8)
    def _(s):
        def forward(part):
            for d in range(2):
                zrecv(d, part, s - 1).wait_recv()
                if steps(d, part) == 8:
                    zcopy(d, part, s).start()
                else:

                    @pl.when(s <= 6)
                    def _():
                        zcopy(d, part, s).start()

                if part == NP:
                    for e in range(2):
                        xcopy(e, at_z((2 * d - 1) * s)).start()

        forward(NP)

        @pl.when(s >= 2)
        def _():
            pass_on(at_z(1 - s))
            pass_on(at_z(s - 1))

        for part in range(NP):
            forward(part)

        @pl.when(s >= 3)
        def _():
            settle(at_z(2 - s))
            settle(at_z(s - 2))

    pass_on(at_z(7))
    finish(1, at_z(7)).start()
    pass_on(at_z(-7))
    finish(0, at_z(-7)).start()
    for d in (6, -6, 7):
        settle(at_z(d))
    finish(2, at_z(7)).start()
    settle(at_z(-7))

    yown[...] = yacc[...].astype(BF16)

    def ycopy(i):
        to = at_z(4 - 8 * i)
        away = yown.at[pl.ds(pl.multiple_of(COLS * lax.div(to, 8), COLS), COLS)]
        return remote(away, ycat.at[zh], ys.at[i], yr.at[i], dev(x, y, to, k))

    def yrecv(i):
        h = lax.div(at_z(8 * i - 4), 8)
        return remote(yown.at[pl.ds(0, COLS)], ycat.at[h], ys.at[i], yr.at[i], dev(x, y, at_z(4 - 8 * i), k))

    ycopy(0).start()
    ycopy(1).start()

    for part in range(NP):
        zrecv(0, part, 7).wait_recv()
    zrecv(1, NP, 7).wait_recv()
    for i in range(3):
        finish(i, at_z(8)).wait_recv()
        finish(i, at_z(-7 if i == 0 else 7)).wait_send()

    @pl.loop(1, 8)
    def _(j):
        for d in range(2):
            for b in (at_z(j), at_z(-j)):
                xcopy(d, b).wait_send()
                fcopy(d, b).wait_send()

    for d in range(2):
        for part in range(NP + 1):

            @pl.loop(0, steps(d, part))
            def _(s):
                zcopy(d, part, s).wait_send()

    for i in range(2):
        yrecv(i).wait_recv()
        ycopy(i).wait_send()

    sibling = dev(x, y, z, 1 - k)

    def all_reduce(rnd, block, arrive):
        def core_part(o):
            q = at_y(o)
            return remote(ubuf.at[2 * q + 1 - k], cbuf.at[rnd, q], cs.at[rnd, q], cr.at[rnd, q], sibling)

        def ring_part(o):
            q = at_y(o)
            return remote(ubuf.at[2 * q + k], rbuf.at[rnd, y], us.at[rnd, q], ur.at[rnd, y], dev(x, q, z, k))

        def ring_part_from(o):
            q = at_y(o)
            return remote(ubuf.at[2 * q + k], rbuf.at[rnd, q], us.at[rnd, q], ur.at[rnd, q], dev(x, q, z, k))

        def ring_whole(o):
            q = at_y(o)
            ref = img.at[rnd, me]
            return remote(ref, ref, gs.at[rnd, q], gr.at[rnd, y], dev(x, q, z, k))

        def ring_whole_from(o):
            q = at_y(o)
            ref = img.at[rnd, 2 * q + k]
            return remote(ref, ref, gs.at[rnd, q], gr.at[rnd, q], dev(x, q, z, k))

        def core_whole(o):
            q = at_y(o)
            ref = img.at[rnd, 2 * q + k]
            return remote(ref, ref, hs.at[rnd, q], hr.at[rnd, q], sibling)

        def core_whole_from(o):
            q = at_y(o)
            ref = img.at[rnd, 2 * q + 1 - k]
            return remote(ref, ref, hs.at[rnd, q], hr.at[rnd, q], sibling)

        def give(o):
            b = 2 * at_y(o) + 1 - k
            ubuf[b] = block(b)
            core_part(o).start()

        def keep(o):
            q = at_y(o)
            b = 2 * q + k
            mine = block(b)
            remote(ubuf.at[b], cbuf.at[rnd, q], cs.at[rnd, q], cr.at[rnd, q], sibling).wait_recv()
            if o:
                ubuf[b] = mine + cbuf[rnd, q]
                ring_part(o).start()
            else:
                img[rnd, me] = mine + cbuf[rnd, q]

        give(2)
        give(1)
        keep(2)
        give(3)
        keep(1)
        give(0)
        keep(3)
        keep(0)
        for o in (1, 3, 2):
            ring_part_from(o).wait_recv()
        img[rnd, me] += rbuf[rnd, at_y(1)] + rbuf[rnd, at_y(3)] + rbuf[rnd, at_y(2)]
        for o in (2, 1, 3):
            ring_whole(o).start()
        core_whole(0).start()
        arrive(me)
        core_whole_from(0).wait_recv()
        arrive(2 * y + 1 - k)
        for o in (1, 3, 2):
            ring_whole_from(o).wait_recv()
            core_whole(o).start()
            arrive(2 * at_y(o) + k)
        for o in (1, 3, 2):
            core_whole_from(o).wait_recv()
            arrive(2 * at_y(o) + 1 - k)
        for o in range(4):
            core_part(o).wait_send()
            core_whole(o).wait_send()
            if o:
                ring_part(o).wait_send()
                ring_whole(o).wait_send()

    def split(v):
        hi = v.astype(BF16)
        return hi, (v - hi.astype(F32)).astype(BF16)

    def tokens_times(v, b):
        both = jnp.concatenate(split(v), axis=0)
        for h in range(2):
            vacc[h] += lax.dot_general(
                both, abuf[8 * h + b], (((1,), (1,)), ((), ())), preferred_element_type=F32
            )

    def products(h):
        return vacc[h, :COLS] + vacc[h, COLS:]

    def set_tokens(h, v):
        hi, lo = split(v)
        thl[h, pl.ds(0, COLS)] = hi
        thl[h, pl.ds(COLS, COLS)] = lo

    def rhs_block(b):
        return jnp.dot(ycat[0], abuf[b], preferred_element_type=F32) + jnp.dot(
            ycat[1], abuf[8 + b], preferred_element_type=F32
        )

    def image_block(b):
        both = jnp.dot(thl[0], abuf[b], preferred_element_type=F32) + jnp.dot(
            thl[1], abuf[8 + b], preferred_element_type=F32
        )
        return both[:COLS] + both[COLS:]

    def column_sum(term):
        acc = jnp.zeros((COLS, 128), F32)
        for b in range(8):
            acc = acc + fold(term(b))
        return total_of(acc)

    def arrived(rnd, direction):
        dots[...] = jnp.zeros_like(dots)

        def go(b):
            v = img[rnd, b]
            tokens_times(v, b)
            dots[...] += fold(v * direction(b))

        return go

    vacc[...] = jnp.zeros_like(vacc)
    all_reduce(0, rhs_block, arrived(0, lambda b: img[0, b]))
    norm = total_of(dots[...])
    for h in range(2):
        t = products(h)
        set_tokens(h, t)
        tok[0, h] = t
        tok[1, h] = t
    vacc[...] = jnp.zeros_like(vacc)
    all_reduce(1, image_block, arrived(1, lambda b: img[0, b]))
    alpha0 = norm / total_of(dots[...])
    for b in range(8):
        res[b] = img[0, b] - alpha0 * img[1, b]
    norm1 = column_sum(lambda b: res[b] * res[b])
    beta = norm1 / norm
    for h in range(2):
        t = tok[1, h] - alpha0 * products(h)
        tok[1, h] = t
        t = t + beta * tok[0, h]
        tok[0, h] = t
        set_tokens(h, t)
    for b in range(8):
        dir1[b] = res[b] + beta * img[0, b]
    vacc[...] = jnp.zeros_like(vacc)
    all_reduce(2, image_block, arrived(2, lambda b: dir1[b]))
    alpha1 = norm1 / total_of(dots[...])
    for b in range(8):
        res[b] = res[b] - alpha1 * img[2, b]
    norm2 = column_sum(lambda b: res[b] * res[b])
    beta = norm2 / norm1
    square = jnp.zeros((COLS, 128), F32)
    for h in range(2):
        t = tok[1, h] - alpha1 * products(h) + beta * tok[0, h]
        square = square + fold(t * t)
    diagonal = lax.broadcasted_iota(jnp.int32, (COLS, 128), 0) == lax.broadcasted_iota(jnp.int32, (COLS, 128), 1)
    curv[me] = jnp.sum(jnp.where(diagonal, total_of(square), 0.0), axis=0, keepdims=True)

    def kcopy(b):
        return remote(curv.at[me], curv.at[me], ks.at[b], kr.at[me], member(b))

    def krecv(b):
        return remote(curv.at[b], curv.at[b], ks.at[b], kr.at[b], member(b))

    @pl.loop(1, 8)
    def _(j):
        kcopy(lax.rem(me + j, 8)).start()

    known = alpha0 * img[0, me] + alpha1 * dir1[me]
    last = res[me] + beta * dir1[me]

    @pl.loop(1, 8)
    def _(j):
        b = lax.rem(me + j, 8)
        krecv(b).wait_recv()
        kcopy(b).wait_send()

    curvature = curv[0]
    for b in range(1, 8):
        curvature = curvature + curv[b]
    alpha2 = norm2 / total_of(jnp.where(diagonal, curvature, 0.0))
    merged = known + alpha2 * last

    origin = lax.rem(zl + 4, 8)
    to_y, to_z, to_k = lax.div(origin, 2), 8 * lax.rem(origin, 2) + me, lax.div(x, 2)
    from_y, from_k = lax.div(zl, 2), lax.rem(zl, 2)
    slot = 2 * lax.rem(x, 2) + zh

    def out_self(dx):
        return (dx == x) & (to_y == y) & (to_z == z) & (to_k == k)

    def ocopy(dx):
        return remote(mblk.at[dx], obuf.at[slot], os.at[dx], orr.at[slot], dev(dx, to_y, to_z, to_k))

    for dx in range(4):
        mblk[dx] = merged[:, 128 * dx : 128 * (dx + 1)]

        @pl.when(jnp.logical_not(out_self(dx)))
        def _():
            ocopy(dx).start()

        @pl.when(out_self(dx))
        def _():
            obuf[slot] = mblk[dx]

    for i in range(2):
        for h in range(2):
            q = 2 * i + h
            sx, sz = 2 * k + i, 8 * h + lax.rem(2 * y + zh + 4, 8)
            mine = (sx == x) & (from_y == y) & (sz == z) & (from_k == k)

            @pl.when(jnp.logical_not(mine))
            def _():
                remote(mblk.at[0], obuf.at[q], os.at[0], orr.at[q], dev(sx, from_y, sz, from_k)).wait_recv()

    for dx in range(4):

        @pl.when(jnp.logical_not(out_self(dx)))
        def _():
            ocopy(dx).wait_send()

    for q in range(4):
        out_ref[:, COLS * q : COLS * (q + 1)] = obuf[q].T


def local(activations, weights):
    dma = pltpu.SemaphoreType.DMA
    vmem = pltpu.VMEM
    return pl.pallas_call(
        kernel,
        out_shape=jax.ShapeDtypeStruct((128, 128), F32),
        in_specs=[pl.BlockSpec(memory_space=pl.ANY)] * 2,
        out_specs=pl.BlockSpec(memory_space=pltpu.VMEM),
        scratch_shapes=[
            vmem((16, 512, 512), BF16),
            vmem((2 * COLS, 4096), BF16),
            vmem((2 * COLS, 512), F32),
            vmem((2 * COLS, 512), BF16),
            vmem((2, COLS, 512), BF16),
            vmem((2, 2 * COLS, 512), BF16),
            vmem((8, COLS, 512), F32),
            vmem((3, 4, COLS, 512), F32),
            vmem((3, 4, COLS, 512), F32),
            vmem((3, 8, COLS, 512), F32),
            vmem((8, COLS, 512), F32),
            vmem((8, COLS, 512), F32),
            vmem((2, 2 * COLS, 512), F32),
            vmem((2, 2, COLS, 512), F32),
            vmem((COLS, 128), F32),
            vmem((8, 1, 128), F32),
            vmem((4, COLS, 128), F32),
            vmem((4, COLS, 128), F32),
            dma((2,)),
            dma((2, NP + 1, 8)),
            dma((2, NP + 1, 8)),
            dma((2, 16)),
            dma((2, 16)),
            dma((2, 16)),
            dma((2, 16)),
            dma((3,)),
            dma((3,)),
            dma((2,)),
            dma((2,)),
            dma((3, 4)),
            dma((3, 4)),
            dma((3, 4)),
            dma((3, 4)),
            dma((3, 4)),
            dma((3, 4)),
            dma((3, 4)),
            dma((3, 4)),
            dma((8,)),
            dma((8,)),
            dma((4,)),
            dma((4,)),
        ],
        compiler_params=pltpu.CompilerParams(
            collective_id=0, has_side_effects=True, vmem_limit_bytes=53 * 1024 * 1024 + 512 * 1024
        ),
    )(activations, jnp.swapaxes(weights, 1, 2))


def solution(mesh):
    in_specs = (P("mp", None, "row"), P("mp", None, ("row", "col")))
    out_specs = P(("row", "col"), "mp")
    return jax.shard_map(local, mesh=mesh, in_specs=in_specs, out_specs=out_specs, check_vma=False)
```

```python
import jax
import jax.numpy as jnp
from jax import lax
from jax.experimental import pallas as pl
from jax.experimental.pallas import tpu as pltpu
from jax.sharding import PartitionSpec as P

MESH = pl.DeviceIdType.MESH
F32 = jnp.float32
BF16 = jnp.bfloat16
NZ = (96, 80)
NP = len(NZ)
ZS = sum(NZ)
COLS = 32
CUTS = 2


def fold(v):
    return v[:, :128] + v[:, 128:256] + v[:, 256:384] + v[:, 384:]


def total_of(v):
    return jnp.sum(v, axis=1, keepdims=True)


def kernel(
    a_hbm, w_hbm, out_ref,
    abuf, wbuf, yacc, yown, ycat, thl, ubuf, cbuf, rbuf, img, res, dir1, vacc, tok, dots, curv, mblk, obuf,
    in_sem, zs, zr, xs, xr, es, er, ys, yr, cs, cr, us, ur, gs, gr, hs, hr, ks, kr, os, orr,
):
    mp = lax.axis_index("mp")
    zl = lax.axis_index("row")
    x = lax.axis_index("col")
    y = lax.div(mp, 4)
    zh = lax.rem(lax.div(mp, 2), 2)
    k = lax.rem(mp, 2)
    z = 8 * zh + zl
    me = 2 * y + k

    def dev(dx, dy, dz, dk):
        return (4 * dy + 2 * lax.div(dz, 8) + dk, lax.rem(dz, 8), dx)

    def remote(src, dst, send, recv, device):
        return pltpu.make_async_remote_copy(
            src_ref=src, dst_ref=dst, send_sem=send, recv_sem=recv, device_id=device, device_id_type=MESH
        )

    def at_z(d):
        return lax.rem(z + d + 16, 16)

    def at_x(d):
        return lax.rem(x + d + 4, 4)

    def at_y(d):
        return lax.rem(y + d, 4)

    def member(b):
        return (4 * lax.div(b, 2) + 2 * zh + lax.rem(b, 2), zl, x)

    in_a = pltpu.make_async_copy(a_hbm.at[0], abuf.at[z], in_sem.at[0])
    in_w = pltpu.make_async_copy(w_hbm.at[0], wbuf, in_sem.at[1])
    in_a.start()
    in_w.start()

    barrier = pltpu.get_barrier_semaphore()

    def greet(device):
        pl.semaphore_signal(barrier, inc=1, device_id=device, device_id_type=MESH)

    greet(dev(x, y, at_z(1), k))
    greet(dev(x, y, at_z(-1), k))
    greet(dev(at_x(1), y, z, k))
    greet(dev(at_x(-1), y, z, k))
    greet(dev(at_x(2), y, z, k))

    @pl.loop(1, 8)
    def _(j):
        greet(member(lax.rem(me + j, 8)))

    in_a.wait()
    pl.semaphore_wait(barrier, 12)

    def piece(b, part, shard):
        if part < NP:
            return abuf.at[b, pl.ds(sum(NZ[:part]), NZ[part])]
        return abuf.at[b, pl.ds(ZS, 512 - ZS), pl.ds(pl.multiple_of(128 * shard, 128), 128)]

    def steps(d, part):
        return 8 if (part < NP) == (d == 0) else 7

    def zlink(d, part, s, distance):
        sign = 1 - 2 * d
        ref = piece(at_z(-sign * distance), part, x)
        return remote(ref, ref, zs.at[d, part, s], zr.at[d, part, s], dev(x, y, at_z(sign), k))

    def zcopy(d, part, s):
        return zlink(d, part, s, s)

    def zrecv(d, part, s):
        return zlink(d, part, s, s + 1)

    def xcopy(i, b):
        ref = piece(b, NP, x)
        return remote(ref, ref, xs.at[i, b], xr.at[i, b], dev(at_x((1, -1, 2)[i]), y, z, k))

    def xrecv(i, b):
        ref = piece(b, NP, at_x((-1, 1, 2)[i]))
        return remote(ref, ref, xs.at[i, b], xr.at[i, b], dev(at_x((1, -1, 2)[i]), y, z, k))

    def finish(i, b):
        ref = piece(b, NP, at_x((1, -1, 2)[i]))
        return remote(ref, ref, es.at[i], er.at[i], dev(x, y, at_z(1 if i == 0 else -1), k))

    def project(b):
        w = wbuf[:, pl.ds(pl.multiple_of(512 * lax.rem(b, 8), 512), 512)]
        yacc[...] += lax.dot_general(w, abuf[b], (((1,), (1,)), ((), ())), preferred_element_type=F32)

    def use(b):
        @pl.when(lax.div(b, 8) == zh)
        def _():
            project(b)

    def settle(b):
        for i in range(3):
            xrecv(i, b).wait_recv()
        use(b)

    for part in (NP, *range(NP)):
        for d in range(2):
            zcopy(d, part, 0).start()
    in_w.wait()
    yacc[...] = jnp.zeros_like(yacc)
    project(z)

    @pl.loop(1, 8)
    def _(s):
        def forward(part):
            for d in range(2):
                zrecv(d, part, s - 1).wait_recv()
                if steps(d, part) == 8:
                    zcopy(d, part, s).start()
                else:

                    @pl.when(s <= 6)
                    def _():
                        zcopy(d, part, s).start()

                if part == NP:
                    for i in range(3):
                        xcopy(i, at_z((2 * d - 1) * s)).start()

        forward(NP)

        for part in range(NP):
            forward(part)

        @pl.when(s >= 3)
        def _():
            settle(at_z(2 - s))
            settle(at_z(s - 2))

    for d in (6, -6):
        settle(at_z(d))
    xrecv(0, at_z(7)).wait_recv()
    finish(1, at_z(7)).start()
    xrecv(1, at_z(-7)).wait_recv()
    finish(0, at_z(-7)).start()
    xrecv(2, at_z(7)).wait_recv()
    finish(2, at_z(7)).start()
    xrecv(1, at_z(7)).wait_recv()
    use(at_z(7))
    xrecv(0, at_z(-7)).wait_recv()
    xrecv(2, at_z(-7)).wait_recv()
    use(at_z(-7))

    yown[...] = yacc[...].astype(BF16)

    def ycopy(i):
        to = at_z(4 - 8 * i)
        away = yown.at[pl.ds(pl.multiple_of(COLS * lax.div(to, 8), COLS), COLS)]
        return remote(away, ycat.at[zh], ys.at[i], yr.at[i], dev(x, y, to, k))

    def yrecv(i):
        h = lax.div(at_z(8 * i - 4), 8)
        return remote(yown.at[pl.ds(0, COLS)], ycat.at[h], ys.at[i], yr.at[i], dev(x, y, at_z(4 - 8 * i), k))

    ycopy(0).start()
    ycopy(1).start()

    for part in range(NP):
        zrecv(0, part, 7).wait_recv()
    zrecv(1, NP, 7).wait_recv()
    for i in range(3):
        finish(i, at_z(8)).wait_recv()
        finish(i, at_z(-7 if i == 0 else 7)).wait_send()

    @pl.loop(1, 8)
    def _(j):
        for i in range(3):
            for b in (at_z(j), at_z(-j)):
                xcopy(i, b).wait_send()

    for d in range(2):
        for part in range(NP + 1):

            @pl.loop(0, steps(d, part))
            def _(s):
                zcopy(d, part, s).wait_send()

    for i in range(2):
        yrecv(i).wait_recv()
        ycopy(i).wait_send()

    sibling = dev(x, y, z, 1 - k)

    def all_reduce(rnd, block, arrive):
        def core_part(o):
            q = at_y(o)
            return remote(ubuf.at[2 * q + 1 - k], cbuf.at[rnd, q], cs.at[rnd, q], cr.at[rnd, q], sibling)

        def cut(c):
            return pl.ds(c * (COLS // CUTS), COLS // CUTS)

        def ring_part(o, c):
            q = at_y(o)
            src, dst = ubuf.at[2 * q + k, cut(c)], rbuf.at[rnd, y, cut(c)]
            return remote(src, dst, us.at[rnd, q, c], ur.at[rnd, y, c], dev(x, q, z, k))

        def ring_part_from(o, c):
            q = at_y(o)
            src, dst = ubuf.at[2 * q + k, cut(c)], rbuf.at[rnd, q, cut(c)]
            return remote(src, dst, us.at[rnd, q, c], ur.at[rnd, q, c], dev(x, q, z, k))

        def ring_whole(o, c):
            q = at_y(o)
            ref = img.at[rnd, me, cut(c)]
            return remote(ref, ref, gs.at[rnd, q, c], gr.at[rnd, y, c], dev(x, q, z, k))

        def ring_whole_from(o, c):
            q = at_y(o)
            ref = img.at[rnd, 2 * q + k, cut(c)]
            return remote(ref, ref, gs.at[rnd, q, c], gr.at[rnd, q, c], dev(x, q, z, k))

        def core_whole(o):
            q = at_y(o)
            ref = img.at[rnd, 2 * q + k]
            return remote(ref, ref, hs.at[rnd, q], hr.at[rnd, q], sibling)

        def core_whole_from(o):
            q = at_y(o)
            ref = img.at[rnd, 2 * q + 1 - k]
            return remote(ref, ref, hs.at[rnd, q], hr.at[rnd, q], sibling)

        def give(o):
            b = 2 * at_y(o) + 1 - k
            ubuf[b] = block(b)
            core_part(o).start()

        def keep(o):
            q = at_y(o)
            b = 2 * q + k
            mine = block(b)
            remote(ubuf.at[b], cbuf.at[rnd, q], cs.at[rnd, q], cr.at[rnd, q], sibling).wait_recv()
            if o:
                ubuf[b] = mine + cbuf[rnd, q]
                ring_part(o, 0).start()
            else:
                img[rnd, me] = mine + cbuf[rnd, q]

        give(2)
        give(1)
        keep(2)
        give(3)
        keep(1)
        give(0)
        keep(3)
        for c in range(1, CUTS):
            for o in (2, 1, 3):
                ring_part(o, c).start()
        keep(0)
        for c in range(CUTS):
            for o in (1, 3, 2):
                ring_part_from(o, c).wait_recv()
            img[rnd, me, cut(c)] += (
                rbuf[rnd, at_y(1), cut(c)] + rbuf[rnd, at_y(3), cut(c)] + rbuf[rnd, at_y(2), cut(c)]
            )
            for o in (2, 1, 3):
                ring_whole(o, c).start()
        core_whole(0).start()
        arrive(me)
        core_whole_from(0).wait_recv()
        arrive(2 * y + 1 - k)
        for o in (1, 3, 2):
            for c in range(CUTS):
                ring_whole_from(o, c).wait_recv()
            core_whole(o).start()
            arrive(2 * at_y(o) + k)
        for o in (1, 3, 2):
            core_whole_from(o).wait_recv()
            arrive(2 * at_y(o) + 1 - k)
        for o in range(4):
            core_part(o).wait_send()
            core_whole(o).wait_send()
            if o:
                for c in range(CUTS):
                    ring_part(o, c).wait_send()
                    ring_whole(o, c).wait_send()

    def split(v):
        hi = v.astype(BF16)
        return hi, (v - hi.astype(F32)).astype(BF16)

    def tokens_times(v, b):
        both = jnp.concatenate(split(v), axis=0)
        for h in range(2):
            vacc[h] += lax.dot_general(
                both, abuf[8 * h + b], (((1,), (1,)), ((), ())), preferred_element_type=F32
            )

    def products(h):
        return vacc[h, :COLS] + vacc[h, COLS:]

    def set_tokens(h, v):
        hi, lo = split(v)
        thl[h, pl.ds(0, COLS)] = hi
        thl[h, pl.ds(COLS, COLS)] = lo

    def rhs_block(b):
        return jnp.dot(ycat[0], abuf[b], preferred_element_type=F32) + jnp.dot(
            ycat[1], abuf[8 + b], preferred_element_type=F32
        )

    def image_block(b):
        both = jnp.dot(thl[0], abuf[b], preferred_element_type=F32) + jnp.dot(
            thl[1], abuf[8 + b], preferred_element_type=F32
        )
        return both[:COLS] + both[COLS:]

    def column_sum(term):
        acc = jnp.zeros((COLS, 128), F32)
        for b in range(8):
            acc = acc + fold(term(b))
        return total_of(acc)

    def arrived(rnd, direction):
        dots[...] = jnp.zeros_like(dots)

        def go(b):
            v = img[rnd, b]
            tokens_times(v, b)
            dots[...] += fold(v * direction(b))

        return go

    vacc[...] = jnp.zeros_like(vacc)
    all_reduce(0, rhs_block, arrived(0, lambda b: img[0, b]))
    norm = total_of(dots[...])
    for h in range(2):
        t = products(h)
        set_tokens(h, t)
        tok[0, h] = t
        tok[1, h] = t
    vacc[...] = jnp.zeros_like(vacc)
    all_reduce(1, image_block, arrived(1, lambda b: img[0, b]))
    alpha0 = norm / total_of(dots[...])
    for b in range(8):
        res[b] = img[0, b] - alpha0 * img[1, b]
    norm1 = column_sum(lambda b: res[b] * res[b])
    beta = norm1 / norm
    for h in range(2):
        t = tok[1, h] - alpha0 * products(h)
        tok[1, h] = t
        t = t + beta * tok[0, h]
        tok[0, h] = t
        set_tokens(h, t)
    for b in range(8):
        dir1[b] = res[b] + beta * img[0, b]
    vacc[...] = jnp.zeros_like(vacc)
    all_reduce(2, image_block, arrived(2, lambda b: dir1[b]))
    alpha1 = norm1 / total_of(dots[...])
    for b in range(8):
        res[b] = res[b] - alpha1 * img[2, b]
    norm2 = column_sum(lambda b: res[b] * res[b])
    beta = norm2 / norm1
    square = jnp.zeros((COLS, 128), F32)
    for h in range(2):
        t = tok[1, h] - alpha1 * products(h) + beta * tok[0, h]
        square = square + fold(t * t)
    diagonal = lax.broadcasted_iota(jnp.int32, (COLS, 128), 0) == lax.broadcasted_iota(jnp.int32, (COLS, 128), 1)
    curv[me] = jnp.sum(jnp.where(diagonal, total_of(square), 0.0), axis=0, keepdims=True)

    def kcopy(b):
        return remote(curv.at[me], curv.at[me], ks.at[b], kr.at[me], member(b))

    def krecv(b):
        return remote(curv.at[b], curv.at[b], ks.at[b], kr.at[b], member(b))

    @pl.loop(1, 8)
    def _(j):
        kcopy(lax.rem(me + j, 8)).start()

    known = alpha0 * img[0, me] + alpha1 * dir1[me]
    last = res[me] + beta * dir1[me]

    @pl.loop(1, 8)
    def _(j):
        b = lax.rem(me + j, 8)
        krecv(b).wait_recv()
        kcopy(b).wait_send()

    curvature = curv[0]
    for b in range(1, 8):
        curvature = curvature + curv[b]
    alpha2 = norm2 / total_of(jnp.where(diagonal, curvature, 0.0))
    merged = known + alpha2 * last

    origin = lax.rem(zl + 4, 8)
    to_y, to_z, to_k = lax.div(origin, 2), 8 * lax.rem(origin, 2) + me, lax.div(x, 2)
    from_y, from_k = lax.div(zl, 2), lax.rem(zl, 2)
    slot = 2 * lax.rem(x, 2) + zh

    def out_self(dx):
        return (dx == x) & (to_y == y) & (to_z == z) & (to_k == k)

    def ocopy(dx):
        return remote(mblk.at[dx], obuf.at[slot], os.at[dx], orr.at[slot], dev(dx, to_y, to_z, to_k))

    for dx in range(4):
        mblk[dx] = merged[:, 128 * dx : 128 * (dx + 1)]

        @pl.when(jnp.logical_not(out_self(dx)))
        def _():
            ocopy(dx).start()

        @pl.when(out_self(dx))
        def _():
            obuf[slot] = mblk[dx]

    for i in range(2):
        for h in range(2):
            q = 2 * i + h
            sx, sz = 2 * k + i, 8 * h + lax.rem(2 * y + zh + 4, 8)
            mine = (sx == x) & (from_y == y) & (sz == z) & (from_k == k)

            @pl.when(jnp.logical_not(mine))
            def _():
                remote(mblk.at[0], obuf.at[q], os.at[0], orr.at[q], dev(sx, from_y, sz, from_k)).wait_recv()

    for dx in range(4):

        @pl.when(jnp.logical_not(out_self(dx)))
        def _():
            ocopy(dx).wait_send()

    for q in range(4):
        out_ref[:, COLS * q : COLS * (q + 1)] = obuf[q].T


def local(activations, weights):
    dma = pltpu.SemaphoreType.DMA
    vmem = pltpu.VMEM
    return pl.pallas_call(
        kernel,
        out_shape=jax.ShapeDtypeStruct((128, 128), F32),
        in_specs=[pl.BlockSpec(memory_space=pl.ANY)] * 2,
        out_specs=pl.BlockSpec(memory_space=pltpu.VMEM),
        scratch_shapes=[
            vmem((16, 512, 512), BF16),
            vmem((2 * COLS, 4096), BF16),
            vmem((2 * COLS, 512), F32),
            vmem((2 * COLS, 512), BF16),
            vmem((2, COLS, 512), BF16),
            vmem((2, 2 * COLS, 512), BF16),
            vmem((8, COLS, 512), F32),
            vmem((3, 4, COLS, 512), F32),
            vmem((3, 4, COLS, 512), F32),
            vmem((3, 8, COLS, 512), F32),
            vmem((8, COLS, 512), F32),
            vmem((8, COLS, 512), F32),
            vmem((2, 2 * COLS, 512), F32),
            vmem((2, 2, COLS, 512), F32),
            vmem((COLS, 128), F32),
            vmem((8, 1, 128), F32),
            vmem((4, COLS, 128), F32),
            vmem((4, COLS, 128), F32),
            dma((2,)),
            dma((2, NP + 1, 8)),
            dma((2, NP + 1, 8)),
            dma((3, 16)),
            dma((3, 16)),
            dma((3,)),
            dma((3,)),
            dma((2,)),
            dma((2,)),
            dma((3, 4)),
            dma((3, 4)),
            dma((3, 4, CUTS)),
            dma((3, 4, CUTS)),
            dma((3, 4, CUTS)),
            dma((3, 4, CUTS)),
            dma((3, 4)),
            dma((3, 4)),
            dma((8,)),
            dma((8,)),
            dma((4,)),
            dma((4,)),
        ],
        compiler_params=pltpu.CompilerParams(
            collective_id=0, has_side_effects=True, vmem_limit_bytes=53 * 1024 * 1024 + 512 * 1024
        ),
    )(activations, jnp.swapaxes(weights, 1, 2))


def solution(mesh):
    in_specs = (P("mp", None, "row"), P("mp", None, ("row", "col")))
    out_specs = P(("row", "col"), "mp")
    return jax.shard_map(local, mesh=mesh, in_specs=in_specs, out_specs=out_specs, check_vma=False)
```

```python
import jax
import jax.numpy as jnp
from jax import lax
from jax.experimental import pallas as pl
from jax.experimental.pallas import tpu as pltpu
from jax.sharding import PartitionSpec as P

MESH = pl.DeviceIdType.MESH
F32 = jnp.float32
BF16 = jnp.bfloat16
NZ = (96, 80)
NP = len(NZ)
ZS = sum(NZ)
HALF = 176
COLS = 32
CUTS = 2


def fold(v):
    return v[:, :128] + v[:, 128:256] + v[:, 256:384] + v[:, 384:]


def total_of(v):
    return jnp.sum(v, axis=1, keepdims=True)


def kernel(
    a_hbm, w_hbm, out_ref,
    abuf, wbuf, yacc, yown, ycat, thl, ubuf, cbuf, rbuf, img, res, dir1, vacc, tok, dots, curv, mblk, obuf,
    in_sem, zs, zr, xs, xr, fs, fr, es, er, ys, yr, cs, cr, us, ur, gs, gr, hs, hr, ks, kr, os, orr,
):
    mp = lax.axis_index("mp")
    zl = lax.axis_index("row")
    x = lax.axis_index("col")
    y = lax.div(mp, 4)
    zh = lax.rem(lax.div(mp, 2), 2)
    k = lax.rem(mp, 2)
    z = 8 * zh + zl
    me = 2 * y + k

    def dev(dx, dy, dz, dk):
        return (4 * dy + 2 * lax.div(dz, 8) + dk, lax.rem(dz, 8), dx)

    def remote(src, dst, send, recv, device):
        return pltpu.make_async_remote_copy(
            src_ref=src, dst_ref=dst, send_sem=send, recv_sem=recv, device_id=device, device_id_type=MESH
        )

    def at_z(d):
        return lax.rem(z + d + 16, 16)

    def at_x(d):
        return lax.rem(x + d + 4, 4)

    def at_y(d):
        return lax.rem(y + d, 4)

    def member(b):
        return (4 * lax.div(b, 2) + 2 * zh + lax.rem(b, 2), zl, x)

    in_a = pltpu.make_async_copy(a_hbm.at[0], abuf.at[z], in_sem.at[0])
    in_w = pltpu.make_async_copy(w_hbm.at[0], wbuf, in_sem.at[1])
    in_a.start()
    in_w.start()

    barrier = pltpu.get_barrier_semaphore()

    def greet(device):
        pl.semaphore_signal(barrier, inc=1, device_id=device, device_id_type=MESH)

    greet(dev(x, y, at_z(1), k))
    greet(dev(x, y, at_z(-1), k))
    greet(dev(at_x(1), y, z, k))
    greet(dev(at_x(-1), y, z, k))

    @pl.loop(1, 8)
    def _(j):
        greet(member(lax.rem(me + j, 8)))

    in_a.wait()
    pl.semaphore_wait(barrier, 11)

    def piece(b, part, shard):
        if part < NP:
            return abuf.at[b, pl.ds(sum(NZ[:part]), NZ[part])]
        return abuf.at[b, pl.ds(ZS, 512 - ZS), pl.ds(pl.multiple_of(128 * shard, 128), 128)]

    def half_piece(b, d, shard):
        rows = pl.ds(ZS, HALF) if d == 0 else pl.ds(ZS + HALF, 512 - ZS - HALF)
        return abuf.at[b, rows, pl.ds(pl.multiple_of(128 * shard, 128), 128)]

    def steps(d, part):
        return 8 if (part < NP) == (d == 0) else 7

    def zlink(d, part, s, distance):
        sign = 1 - 2 * d
        ref = piece(at_z(-sign * distance), part, x)
        return remote(ref, ref, zs.at[d, part, s], zr.at[d, part, s], dev(x, y, at_z(sign), k))

    def zcopy(d, part, s):
        return zlink(d, part, s, s)

    def zrecv(d, part, s):
        return zlink(d, part, s, s + 1)

    def xcopy(d, b):
        ref = piece(b, NP, x)
        return remote(ref, ref, xs.at[d, b], xr.at[d, b], dev(at_x(1 - 2 * d), y, z, k))

    def xrecv(d, b):
        ref = piece(b, NP, at_x(2 * d - 1))
        return remote(ref, ref, xs.at[d, b], xr.at[d, b], dev(at_x(1 - 2 * d), y, z, k))

    def fcopy(d, b):
        ref = half_piece(b, d, at_x(2 * d - 1))
        return remote(ref, ref, fs.at[d, b], fr.at[d, b], dev(at_x(1 - 2 * d), y, z, k))

    def frecv(d, b):
        ref = half_piece(b, d, at_x(2))
        return remote(ref, ref, fs.at[d, b], fr.at[d, b], dev(at_x(1 - 2 * d), y, z, k))

    def finish(i, b):
        ref = piece(b, NP, at_x((1, -1, 2)[i]))
        return remote(ref, ref, es.at[i], er.at[i], dev(x, y, at_z(1 if i == 0 else -1), k))

    def pass_on(b):
        for d in range(2):
            xrecv(d, b).wait_recv()
            fcopy(d, b).start()

    def project(b):
        w = wbuf[:, pl.ds(pl.multiple_of(512 * lax.rem(b, 8), 512), 512)]
        yacc[...] += lax.dot_general(w, abuf[b], (((1,), (1,)), ((), ())), preferred_element_type=F32)

    def settle(b):
        for d in range(2):
            frecv(d, b).wait_recv()

        @pl.when(lax.div(b, 8) == zh)
        def _():
            project(b)

    for part in (NP, *range(NP)):
        for d in range(2):
            zcopy(d, part, 0).start()
    in_w.wait()
    yacc[...] = jnp.zeros_like(yacc)
    project(z)

    @pl.loop(1, 8)
    def _(s):
        def forward(part):
            for d in range(2):
                zrecv(d, part, s - 1).wait_recv()
                if steps(d, part) == 8:
                    zcopy(d, part, s).start()
                else:

                    @pl.when(s <= 6)
                    def _():
                        zcopy(d, part, s).start()

                if part == NP:
                    for e in range(2):
                        xcopy(e, at_z((2 * d - 1) * s)).start()

        forward(NP)

        @pl.when(s >= 2)
        def _():
            pass_on(at_z(1 - s))
            pass_on(at_z(s - 1))

        for part in range(NP):
            forward(part)

        @pl.when(s >= 3)
        def _():
            settle(at_z(2 - s))
            settle(at_z(s - 2))

    pass_on(at_z(7))
    finish(1, at_z(7)).start()
    pass_on(at_z(-7))
    finish(0, at_z(-7)).start()
    for d in (6, -6, 7):
        settle(at_z(d))
    finish(2, at_z(7)).start()
    settle(at_z(-7))

    yown[...] = yacc[...].astype(BF16)

    def ycopy(i):
        to = at_z(4 - 8 * i)
        away = yown.at[pl.ds(pl.multiple_of(COLS * lax.div(to, 8), COLS), COLS)]
        return remote(away, ycat.at[zh], ys.at[i], yr.at[i], dev(x, y, to, k))

    def yrecv(i):
        h = lax.div(at_z(8 * i - 4), 8)
        return remote(yown.at[pl.ds(0, COLS)], ycat.at[h], ys.at[i], yr.at[i], dev(x, y, at_z(4 - 8 * i), k))

    ycopy(0).start()
    ycopy(1).start()

    for part in range(NP):
        zrecv(0, part, 7).wait_recv()
    zrecv(1, NP, 7).wait_recv()
    for i in range(3):
        finish(i, at_z(8)).wait_recv()
        finish(i, at_z(-7 if i == 0 else 7)).wait_send()

    @pl.loop(1, 8)
    def _(j):
        for d in range(2):
            for b in (at_z(j), at_z(-j)):
                xcopy(d, b).wait_send()
                fcopy(d, b).wait_send()

    for d in range(2):
        for part in range(NP + 1):

            @pl.loop(0, steps(d, part))
            def _(s):
                zcopy(d, part, s).wait_send()

    for i in range(2):
        yrecv(i).wait_recv()
        ycopy(i).wait_send()

    sibling = dev(x, y, z, 1 - k)

    def all_reduce(rnd, block, arrive):
        def core_part(o):
            q = at_y(o)
            return remote(ubuf.at[2 * q + 1 - k], cbuf.at[rnd, q], cs.at[rnd, q], cr.at[rnd, q], sibling)

        def cut(c):
            return pl.ds(c * (COLS // CUTS), COLS // CUTS)

        def ring_part(o, c):
            q = at_y(o)
            src, dst = ubuf.at[2 * q + k, cut(c)], rbuf.at[rnd, y, cut(c)]
            return remote(src, dst, us.at[rnd, q, c], ur.at[rnd, y, c], dev(x, q, z, k))

        def ring_part_from(o, c):
            q = at_y(o)
            src, dst = ubuf.at[2 * q + k, cut(c)], rbuf.at[rnd, q, cut(c)]
            return remote(src, dst, us.at[rnd, q, c], ur.at[rnd, q, c], dev(x, q, z, k))

        def ring_whole(o, c):
            q = at_y(o)
            ref = img.at[rnd, me, cut(c)]
            return remote(ref, ref, gs.at[rnd, q, c], gr.at[rnd, y, c], dev(x, q, z, k))

        def ring_whole_from(o, c):
            q = at_y(o)
            ref = img.at[rnd, 2 * q + k, cut(c)]
            return remote(ref, ref, gs.at[rnd, q, c], gr.at[rnd, q, c], dev(x, q, z, k))

        def core_whole(o):
            q = at_y(o)
            ref = img.at[rnd, 2 * q + k]
            return remote(ref, ref, hs.at[rnd, q], hr.at[rnd, q], sibling)

        def core_whole_from(o):
            q = at_y(o)
            ref = img.at[rnd, 2 * q + 1 - k]
            return remote(ref, ref, hs.at[rnd, q], hr.at[rnd, q], sibling)

        def give(o):
            b = 2 * at_y(o) + 1 - k
            ubuf[b] = block(b)
            core_part(o).start()

        def keep(o):
            q = at_y(o)
            b = 2 * q + k
            mine = block(b)
            remote(ubuf.at[b], cbuf.at[rnd, q], cs.at[rnd, q], cr.at[rnd, q], sibling).wait_recv()
            if o:
                ubuf[b] = mine + cbuf[rnd, q]
                ring_part(o, 0).start()
            else:
                img[rnd, me] = mine + cbuf[rnd, q]

        give(2)
        give(1)
        keep(2)
        give(3)
        keep(1)
        give(0)
        keep(3)
        for c in range(1, CUTS):
            for o in (2, 1, 3):
                ring_part(o, c).start()
        keep(0)
        for c in range(CUTS):
            for o in (1, 3, 2):
                ring_part_from(o, c).wait_recv()
            img[rnd, me, cut(c)] += (
                rbuf[rnd, at_y(1), cut(c)] + rbuf[rnd, at_y(3), cut(c)] + rbuf[rnd, at_y(2), cut(c)]
            )
            for o in (2, 1, 3):
                ring_whole(o, c).start()
        core_whole(0).start()
        arrive(me)
        core_whole_from(0).wait_recv()
        arrive(2 * y + 1 - k)
        for o in (1, 3, 2):
            for c in range(CUTS):
                ring_whole_from(o, c).wait_recv()
            core_whole(o).start()
            arrive(2 * at_y(o) + k)
        for o in (1, 3, 2):
            core_whole_from(o).wait_recv()
            arrive(2 * at_y(o) + 1 - k)
        for o in range(4):
            core_part(o).wait_send()
            core_whole(o).wait_send()
            if o:
                for c in range(CUTS):
                    ring_part(o, c).wait_send()
                    ring_whole(o, c).wait_send()

    def split(v):
        hi = v.astype(BF16)
        return hi, (v - hi.astype(F32)).astype(BF16)

    def tokens_times(v, b):
        both = jnp.concatenate(split(v), axis=0)
        for h in range(2):
            vacc[h] += lax.dot_general(
                both, abuf[8 * h + b], (((1,), (1,)), ((), ())), preferred_element_type=F32
            )

    def products(h):
        return vacc[h, :COLS] + vacc[h, COLS:]

    def set_tokens(h, v):
        hi, lo = split(v)
        thl[h, pl.ds(0, COLS)] = hi
        thl[h, pl.ds(COLS, COLS)] = lo

    def rhs_block(b):
        return jnp.dot(ycat[0], abuf[b], preferred_element_type=F32) + jnp.dot(
            ycat[1], abuf[8 + b], preferred_element_type=F32
        )

    def image_block(b):
        both = jnp.dot(thl[0], abuf[b], preferred_element_type=F32) + jnp.dot(
            thl[1], abuf[8 + b], preferred_element_type=F32
        )
        return both[:COLS] + both[COLS:]

    def column_sum(term):
        acc = jnp.zeros((COLS, 128), F32)
        for b in range(8):
            acc = acc + fold(term(b))
        return total_of(acc)

    def arrived(rnd, direction):
        dots[...] = jnp.zeros_like(dots)

        def go(b):
            v = img[rnd, b]
            tokens_times(v, b)
            dots[...] += fold(v * direction(b))

        return go

    vacc[...] = jnp.zeros_like(vacc)
    all_reduce(0, rhs_block, arrived(0, lambda b: img[0, b]))
    norm = total_of(dots[...])
    for h in range(2):
        t = products(h)
        set_tokens(h, t)
        tok[0, h] = t
        tok[1, h] = t
    vacc[...] = jnp.zeros_like(vacc)
    all_reduce(1, image_block, arrived(1, lambda b: img[0, b]))
    alpha0 = norm / total_of(dots[...])
    for b in range(8):
        res[b] = img[0, b] - alpha0 * img[1, b]
    norm1 = column_sum(lambda b: res[b] * res[b])
    beta = norm1 / norm
    for h in range(2):
        t = tok[1, h] - alpha0 * products(h)
        tok[1, h] = t
        t = t + beta * tok[0, h]
        tok[0, h] = t
        set_tokens(h, t)
    for b in range(8):
        dir1[b] = res[b] + beta * img[0, b]
    vacc[...] = jnp.zeros_like(vacc)
    all_reduce(2, image_block, arrived(2, lambda b: dir1[b]))
    alpha1 = norm1 / total_of(dots[...])
    for b in range(8):
        res[b] = res[b] - alpha1 * img[2, b]
    norm2 = column_sum(lambda b: res[b] * res[b])
    beta = norm2 / norm1
    square = jnp.zeros((COLS, 128), F32)
    for h in range(2):
        t = tok[1, h] - alpha1 * products(h) + beta * tok[0, h]
        square = square + fold(t * t)
    diagonal = lax.broadcasted_iota(jnp.int32, (COLS, 128), 0) == lax.broadcasted_iota(jnp.int32, (COLS, 128), 1)
    curv[me] = jnp.sum(jnp.where(diagonal, total_of(square), 0.0), axis=0, keepdims=True)

    def kcopy(b):
        return remote(curv.at[me], curv.at[me], ks.at[b], kr.at[me], member(b))

    def krecv(b):
        return remote(curv.at[b], curv.at[b], ks.at[b], kr.at[b], member(b))

    @pl.loop(1, 8)
    def _(j):
        kcopy(lax.rem(me + j, 8)).start()

    known = alpha0 * img[0, me] + alpha1 * dir1[me]
    last = res[me] + beta * dir1[me]

    @pl.loop(1, 8)
    def _(j):
        b = lax.rem(me + j, 8)
        krecv(b).wait_recv()
        kcopy(b).wait_send()

    curvature = curv[0]
    for b in range(1, 8):
        curvature = curvature + curv[b]
    alpha2 = norm2 / total_of(jnp.where(diagonal, curvature, 0.0))
    merged = known + alpha2 * last

    origin = lax.rem(zl + 4, 8)
    to_y, to_z, to_k = lax.div(origin, 2), 8 * lax.rem(origin, 2) + me, lax.div(x, 2)
    from_y, from_k = lax.div(zl, 2), lax.rem(zl, 2)
    slot = 2 * lax.rem(x, 2) + zh

    def out_self(dx):
        return (dx == x) & (to_y == y) & (to_z == z) & (to_k == k)

    def ocopy(dx):
        return remote(mblk.at[dx], obuf.at[slot], os.at[dx], orr.at[slot], dev(dx, to_y, to_z, to_k))

    for dx in range(4):
        mblk[dx] = merged[:, 128 * dx : 128 * (dx + 1)]

        @pl.when(jnp.logical_not(out_self(dx)))
        def _():
            ocopy(dx).start()

        @pl.when(out_self(dx))
        def _():
            obuf[slot] = mblk[dx]

    for i in range(2):
        for h in range(2):
            q = 2 * i + h
            sx, sz = 2 * k + i, 8 * h + lax.rem(2 * y + zh + 4, 8)
            mine = (sx == x) & (from_y == y) & (sz == z) & (from_k == k)

            @pl.when(jnp.logical_not(mine))
            def _():
                remote(mblk.at[0], obuf.at[q], os.at[0], orr.at[q], dev(sx, from_y, sz, from_k)).wait_recv()

    for dx in range(4):

        @pl.when(jnp.logical_not(out_self(dx)))
        def _():
            ocopy(dx).wait_send()

    for q in range(4):
        out_ref[:, COLS * q : COLS * (q + 1)] = obuf[q].T


def local(activations, weights):
    dma = pltpu.SemaphoreType.DMA
    vmem = pltpu.VMEM
    return pl.pallas_call(
        kernel,
        out_shape=jax.ShapeDtypeStruct((128, 128), F32),
        in_specs=[pl.BlockSpec(memory_space=pl.ANY)] * 2,
        out_specs=pl.BlockSpec(memory_space=pltpu.VMEM),
        scratch_shapes=[
            vmem((16, 512, 512), BF16),
            vmem((2 * COLS, 4096), BF16),
            vmem((2 * COLS, 512), F32),
            vmem((2 * COLS, 512), BF16),
            vmem((2, COLS, 512), BF16),
            vmem((2, 2 * COLS, 512), BF16),
            vmem((8, COLS, 512), F32),
            vmem((3, 4, COLS, 512), F32),
            vmem((3, 4, COLS, 512), F32),
            vmem((3, 8, COLS, 512), F32),
            vmem((8, COLS, 512), F32),
            vmem((8, COLS, 512), F32),
            vmem((2, 2 * COLS, 512), F32),
            vmem((2, 2, COLS, 512), F32),
            vmem((COLS, 128), F32),
            vmem((8, 1, 128), F32),
            vmem((4, COLS, 128), F32),
            vmem((4, COLS, 128), F32),
            dma((2,)),
            dma((2, NP + 1, 8)),
            dma((2, NP + 1, 8)),
            dma((2, 16)),
            dma((2, 16)),
            dma((2, 16)),
            dma((2, 16)),
            dma((3,)),
            dma((3,)),
            dma((2,)),
            dma((2,)),
            dma((3, 4)),
            dma((3, 4)),
            dma((3, 4, CUTS)),
            dma((3, 4, CUTS)),
            dma((3, 4, CUTS)),
            dma((3, 4, CUTS)),
            dma((3, 4)),
            dma((3, 4)),
            dma((8,)),
            dma((8,)),
            dma((4,)),
            dma((4,)),
        ],
        compiler_params=pltpu.CompilerParams(
            collective_id=0, has_side_effects=True, vmem_limit_bytes=53 * 1024 * 1024 + 512 * 1024
        ),
    )(activations, jnp.swapaxes(weights, 1, 2))


def solution(mesh):
    in_specs = (P("mp", None, "row"), P("mp", None, ("row", "col")))
    out_specs = P(("row", "col"), "mp")
    return jax.shard_map(local, mesh=mesh, in_specs=in_specs, out_specs=out_specs, check_vma=False)
```

```python
import jax
import jax.numpy as jnp
from jax import lax
from jax.experimental import pallas as pl
from jax.experimental.pallas import tpu as pltpu
from jax.sharding import PartitionSpec as P

MESH = pl.DeviceIdType.MESH
F32 = jnp.float32
BF16 = jnp.bfloat16
NZ = (96, 80)
NP = len(NZ)
ZS = sum(NZ)
HALF = 176
COLS = 32
CUTS = 2


def fold(v):
    return v[:, :128] + v[:, 128:256] + v[:, 256:384] + v[:, 384:]


def total_of(v):
    return jnp.sum(v, axis=1, keepdims=True)


def kernel(
    a_hbm, w_hbm, out_ref,
    abuf, wbuf, yacc, yown, ycat, thl, ubuf, cbuf, rbuf, img, res, dir1, vacc, tok, dots, curv, mblk, obuf, narrow_parts, narrow_theirs, narrow_whole,
    in_sem, zs, zr, xs, xr, fs, fr, es, er, ys, yr, cs, cr, us, ur, gs, gr, hs, hr, ks, kr, os, orr,
):
    mp = lax.axis_index("mp")
    zl = lax.axis_index("row")
    x = lax.axis_index("col")
    y = lax.div(mp, 4)
    zh = lax.rem(lax.div(mp, 2), 2)
    k = lax.rem(mp, 2)
    z = 8 * zh + zl
    me = 2 * y + k

    def dev(dx, dy, dz, dk):
        return (4 * dy + 2 * lax.div(dz, 8) + dk, lax.rem(dz, 8), dx)

    def remote(src, dst, send, recv, device):
        return pltpu.make_async_remote_copy(
            src_ref=src, dst_ref=dst, send_sem=send, recv_sem=recv, device_id=device, device_id_type=MESH
        )

    def at_z(d):
        return lax.rem(z + d + 16, 16)

    def at_x(d):
        return lax.rem(x + d + 4, 4)

    def at_y(d):
        return lax.rem(y + d, 4)

    def member(b):
        return (4 * lax.div(b, 2) + 2 * zh + lax.rem(b, 2), zl, x)

    in_a = pltpu.make_async_copy(a_hbm.at[0], abuf.at[z], in_sem.at[0])
    in_w = pltpu.make_async_copy(w_hbm.at[0], wbuf, in_sem.at[1])
    in_a.start()
    in_w.start()

    barrier = pltpu.get_barrier_semaphore()

    def greet(device):
        pl.semaphore_signal(barrier, inc=1, device_id=device, device_id_type=MESH)

    greet(dev(x, y, at_z(1), k))
    greet(dev(x, y, at_z(-1), k))
    greet(dev(at_x(1), y, z, k))
    greet(dev(at_x(-1), y, z, k))

    @pl.loop(1, 8)
    def _(j):
        greet(member(lax.rem(me + j, 8)))

    in_a.wait()
    pl.semaphore_wait(barrier, 11)

    def piece(b, part, shard):
        if part < NP:
            return abuf.at[b, pl.ds(sum(NZ[:part]), NZ[part])]
        return abuf.at[b, pl.ds(ZS, 512 - ZS), pl.ds(pl.multiple_of(128 * shard, 128), 128)]

    def half_piece(b, d, shard):
        rows = pl.ds(ZS, HALF) if d == 0 else pl.ds(ZS + HALF, 512 - ZS - HALF)
        return abuf.at[b, rows, pl.ds(pl.multiple_of(128 * shard, 128), 128)]

    def steps(d, part):
        return 8 if (part < NP) == (d == 0) else 7

    def zlink(d, part, s, distance):
        sign = 1 - 2 * d
        ref = piece(at_z(-sign * distance), part, x)
        return remote(ref, ref, zs.at[d, part, s], zr.at[d, part, s], dev(x, y, at_z(sign), k))

    def zcopy(d, part, s):
        return zlink(d, part, s, s)

    def zrecv(d, part, s):
        return zlink(d, part, s, s + 1)

    def xcopy(d, b):
        ref = piece(b, NP, x)
        return remote(ref, ref, xs.at[d, b], xr.at[d, b], dev(at_x(1 - 2 * d), y, z, k))

    def xrecv(d, b):
        ref = piece(b, NP, at_x(2 * d - 1))
        return remote(ref, ref, xs.at[d, b], xr.at[d, b], dev(at_x(1 - 2 * d), y, z, k))

    def fcopy(d, b):
        ref = half_piece(b, d, at_x(2 * d - 1))
        return remote(ref, ref, fs.at[d, b], fr.at[d, b], dev(at_x(1 - 2 * d), y, z, k))

    def frecv(d, b):
        ref = half_piece(b, d, at_x(2))
        return remote(ref, ref, fs.at[d, b], fr.at[d, b], dev(at_x(1 - 2 * d), y, z, k))

    def finish(i, b):
        ref = piece(b, NP, at_x((1, -1, 2)[i]))
        return remote(ref, ref, es.at[i], er.at[i], dev(x, y, at_z(1 if i == 0 else -1), k))

    def pass_on(b):
        for d in range(2):
            xrecv(d, b).wait_recv()
            fcopy(d, b).start()

    def project(b):
        w = wbuf[:, pl.ds(pl.multiple_of(512 * lax.rem(b, 8), 512), 512)]
        yacc[...] += lax.dot_general(w, abuf[b], (((1,), (1,)), ((), ())), preferred_element_type=F32)

    def settle(b):
        for d in range(2):
            frecv(d, b).wait_recv()

        @pl.when(lax.div(b, 8) == zh)
        def _():
            project(b)

    for part in (NP, *range(NP)):
        for d in range(2):
            zcopy(d, part, 0).start()
    in_w.wait()
    yacc[...] = jnp.zeros_like(yacc)
    project(z)

    @pl.loop(1, 8)
    def _(s):
        def forward(part):
            for d in range(2):
                zrecv(d, part, s - 1).wait_recv()
                if steps(d, part) == 8:
                    zcopy(d, part, s).start()
                else:

                    @pl.when(s <= 6)
                    def _():
                        zcopy(d, part, s).start()

                if part == NP:
                    for e in range(2):
                        xcopy(e, at_z((2 * d - 1) * s)).start()

        forward(NP)

        @pl.when(s >= 2)
        def _():
            pass_on(at_z(1 - s))
            pass_on(at_z(s - 1))

        for part in range(NP):
            forward(part)

        @pl.when(s >= 3)
        def _():
            settle(at_z(2 - s))
            settle(at_z(s - 2))

    pass_on(at_z(7))
    finish(1, at_z(7)).start()
    pass_on(at_z(-7))
    finish(0, at_z(-7)).start()
    for d in (6, -6, 7):
        settle(at_z(d))
    finish(2, at_z(7)).start()
    settle(at_z(-7))

    yown[...] = yacc[...].astype(BF16)

    def ycopy(i):
        to = at_z(4 - 8 * i)
        away = yown.at[pl.ds(pl.multiple_of(COLS * lax.div(to, 8), COLS), COLS)]
        return remote(away, ycat.at[zh], ys.at[i], yr.at[i], dev(x, y, to, k))

    def yrecv(i):
        h = lax.div(at_z(8 * i - 4), 8)
        return remote(yown.at[pl.ds(0, COLS)], ycat.at[h], ys.at[i], yr.at[i], dev(x, y, at_z(4 - 8 * i), k))

    ycopy(0).start()
    ycopy(1).start()

    for part in range(NP):
        zrecv(0, part, 7).wait_recv()
    zrecv(1, NP, 7).wait_recv()
    for i in range(3):
        finish(i, at_z(8)).wait_recv()
        finish(i, at_z(-7 if i == 0 else 7)).wait_send()

    @pl.loop(1, 8)
    def _(j):
        for d in range(2):
            for b in (at_z(j), at_z(-j)):
                xcopy(d, b).wait_send()
                fcopy(d, b).wait_send()

    for d in range(2):
        for part in range(NP + 1):

            @pl.loop(0, steps(d, part))
            def _(s):
                zcopy(d, part, s).wait_send()

    for i in range(2):
        yrecv(i).wait_recv()
        ycopy(i).wait_send()

    sibling = dev(x, y, z, 1 - k)

    def all_reduce(rnd, block, arrive):
        narrow = rnd == 2
        cuts = 1 if narrow else CUTS
        parts = narrow_parts if narrow else ubuf
        theirs = narrow_theirs if narrow else rbuf.at[rnd]
        whole = narrow_whole if narrow else img.at[rnd]

        def core_part(o):
            q = at_y(o)
            return remote(ubuf.at[2 * q + 1 - k], cbuf.at[rnd, q], cs.at[rnd, q], cr.at[rnd, q], sibling)

        def cut(c):
            return pl.ds(c * (COLS // cuts), COLS // cuts)

        def ring_part(o, c):
            q = at_y(o)
            src, dst = parts.at[2 * q + k, cut(c)], theirs.at[y, cut(c)]
            return remote(src, dst, us.at[rnd, q, c], ur.at[rnd, y, c], dev(x, q, z, k))

        def ring_part_from(o, c):
            q = at_y(o)
            src, dst = parts.at[2 * q + k, cut(c)], theirs.at[q, cut(c)]
            return remote(src, dst, us.at[rnd, q, c], ur.at[rnd, q, c], dev(x, q, z, k))

        def ring_whole(o, c):
            q = at_y(o)
            ref = whole.at[me, cut(c)]
            return remote(ref, ref, gs.at[rnd, q, c], gr.at[rnd, y, c], dev(x, q, z, k))

        def ring_whole_from(o, c):
            q = at_y(o)
            ref = whole.at[2 * q + k, cut(c)]
            return remote(ref, ref, gs.at[rnd, q, c], gr.at[rnd, q, c], dev(x, q, z, k))

        def core_whole(o):
            q = at_y(o)
            ref = whole.at[2 * q + k]
            return remote(ref, ref, hs.at[rnd, q], hr.at[rnd, q], sibling)

        def core_whole_from(o):
            q = at_y(o)
            ref = whole.at[2 * q + 1 - k]
            return remote(ref, ref, hs.at[rnd, q], hr.at[rnd, q], sibling)

        def give(o):
            b = 2 * at_y(o) + 1 - k
            ubuf[b] = block(b)
            core_part(o).start()

        def keep(o):
            q = at_y(o)
            b = 2 * q + k
            mine = block(b)
            remote(ubuf.at[b], cbuf.at[rnd, q], cs.at[rnd, q], cr.at[rnd, q], sibling).wait_recv()
            if o:
                parts[b] = (mine + cbuf[rnd, q]).astype(parts.dtype)
                ring_part(o, 0).start()
            else:
                img[rnd, me] = mine + cbuf[rnd, q]

        def widened(b):
            if narrow:
                img[rnd, b] = whole[b].astype(F32)
            arrive(b)

        give(2)
        give(1)
        keep(2)
        give(3)
        keep(1)
        give(0)
        keep(3)
        for c in range(1, cuts):
            for o in (2, 1, 3):
                ring_part(o, c).start()
        keep(0)
        for c in range(cuts):
            for o in (1, 3, 2):
                ring_part_from(o, c).wait_recv()
            total = img[rnd, me, cut(c)] + (
                theirs[at_y(1), cut(c)].astype(F32)
                + theirs[at_y(3), cut(c)].astype(F32)
                + theirs[at_y(2), cut(c)].astype(F32)
            )
            whole[me, cut(c)] = total.astype(whole.dtype)
            for o in (2, 1, 3):
                ring_whole(o, c).start()
        core_whole(0).start()
        widened(me)
        core_whole_from(0).wait_recv()
        widened(2 * y + 1 - k)
        for o in (1, 3, 2):
            for c in range(cuts):
                ring_whole_from(o, c).wait_recv()
            core_whole(o).start()
            widened(2 * at_y(o) + k)
        for o in (1, 3, 2):
            core_whole_from(o).wait_recv()
            widened(2 * at_y(o) + 1 - k)
        for o in range(4):
            core_part(o).wait_send()
            core_whole(o).wait_send()
            if o:
                for c in range(cuts):
                    ring_part(o, c).wait_send()
                    ring_whole(o, c).wait_send()

    def split(v):
        hi = v.astype(BF16)
        return hi, (v - hi.astype(F32)).astype(BF16)

    def tokens_times(v, b):
        both = jnp.concatenate(split(v), axis=0)
        for h in range(2):
            vacc[h] += lax.dot_general(
                both, abuf[8 * h + b], (((1,), (1,)), ((), ())), preferred_element_type=F32
            )

    def products(h):
        return vacc[h, :COLS] + vacc[h, COLS:]

    def set_tokens(h, v):
        hi, lo = split(v)
        thl[h, pl.ds(0, COLS)] = hi
        thl[h, pl.ds(COLS, COLS)] = lo

    def rhs_block(b):
        return jnp.dot(ycat[0], abuf[b], preferred_element_type=F32) + jnp.dot(
            ycat[1], abuf[8 + b], preferred_element_type=F32
        )

    def image_block(b):
        both = jnp.dot(thl[0], abuf[b], preferred_element_type=F32) + jnp.dot(
            thl[1], abuf[8 + b], preferred_element_type=F32
        )
        return both[:COLS] + both[COLS:]

    def column_sum(term):
        acc = jnp.zeros((COLS, 128), F32)
        for b in range(8):
            acc = acc + fold(term(b))
        return total_of(acc)

    def arrived(rnd, direction):
        dots[...] = jnp.zeros_like(dots)

        def go(b):
            v = img[rnd, b]
            tokens_times(v, b)
            dots[...] += fold(v * direction(b))

        return go

    vacc[...] = jnp.zeros_like(vacc)
    all_reduce(0, rhs_block, arrived(0, lambda b: img[0, b]))
    norm = total_of(dots[...])
    for h in range(2):
        t = products(h)
        set_tokens(h, t)
        tok[0, h] = t
        tok[1, h] = t
    vacc[...] = jnp.zeros_like(vacc)
    all_reduce(1, image_block, arrived(1, lambda b: img[0, b]))
    alpha0 = norm / total_of(dots[...])
    for b in range(8):
        res[b] = img[0, b] - alpha0 * img[1, b]
    norm1 = column_sum(lambda b: res[b] * res[b])
    beta = norm1 / norm
    for h in range(2):
        t = tok[1, h] - alpha0 * products(h)
        tok[1, h] = t
        t = t + beta * tok[0, h]
        tok[0, h] = t
        set_tokens(h, t)
    for b in range(8):
        dir1[b] = res[b] + beta * img[0, b]
    vacc[...] = jnp.zeros_like(vacc)
    all_reduce(2, image_block, arrived(2, lambda b: dir1[b]))
    alpha1 = norm1 / total_of(dots[...])
    for b in range(8):
        res[b] = res[b] - alpha1 * img[2, b]
    norm2 = column_sum(lambda b: res[b] * res[b])
    beta = norm2 / norm1
    square = jnp.zeros((COLS, 128), F32)
    for h in range(2):
        t = tok[1, h] - alpha1 * products(h) + beta * tok[0, h]
        square = square + fold(t * t)
    diagonal = lax.broadcasted_iota(jnp.int32, (COLS, 128), 0) == lax.broadcasted_iota(jnp.int32, (COLS, 128), 1)
    curv[me] = jnp.sum(jnp.where(diagonal, total_of(square), 0.0), axis=0, keepdims=True)

    def kcopy(b):
        return remote(curv.at[me], curv.at[me], ks.at[b], kr.at[me], member(b))

    def krecv(b):
        return remote(curv.at[b], curv.at[b], ks.at[b], kr.at[b], member(b))

    @pl.loop(1, 8)
    def _(j):
        kcopy(lax.rem(me + j, 8)).start()

    known = alpha0 * img[0, me] + alpha1 * dir1[me]
    last = res[me] + beta * dir1[me]

    @pl.loop(1, 8)
    def _(j):
        b = lax.rem(me + j, 8)
        krecv(b).wait_recv()
        kcopy(b).wait_send()

    curvature = curv[0]
    for b in range(1, 8):
        curvature = curvature + curv[b]
    alpha2 = norm2 / total_of(jnp.where(diagonal, curvature, 0.0))
    merged = known + alpha2 * last

    origin = lax.rem(zl + 4, 8)
    to_y, to_z, to_k = lax.div(origin, 2), 8 * lax.rem(origin, 2) + me, lax.div(x, 2)
    from_y, from_k = lax.div(zl, 2), lax.rem(zl, 2)
    slot = 2 * lax.rem(x, 2) + zh

    def out_self(dx):
        return (dx == x) & (to_y == y) & (to_z == z) & (to_k == k)

    def ocopy(dx):
        return remote(mblk.at[dx], obuf.at[slot], os.at[dx], orr.at[slot], dev(dx, to_y, to_z, to_k))

    for dx in range(4):
        mblk[dx] = merged[:, 128 * dx : 128 * (dx + 1)]

        @pl.when(jnp.logical_not(out_self(dx)))
        def _():
            ocopy(dx).start()

        @pl.when(out_self(dx))
        def _():
            obuf[slot] = mblk[dx]

    for i in range(2):
        for h in range(2):
            q = 2 * i + h
            sx, sz = 2 * k + i, 8 * h + lax.rem(2 * y + zh + 4, 8)
            mine = (sx == x) & (from_y == y) & (sz == z) & (from_k == k)

            @pl.when(jnp.logical_not(mine))
            def _():
                remote(mblk.at[0], obuf.at[q], os.at[0], orr.at[q], dev(sx, from_y, sz, from_k)).wait_recv()

    for dx in range(4):

        @pl.when(jnp.logical_not(out_self(dx)))
        def _():
            ocopy(dx).wait_send()

    for q in range(4):
        out_ref[:, COLS * q : COLS * (q + 1)] = obuf[q].T


def local(activations, weights):
    dma = pltpu.SemaphoreType.DMA
    vmem = pltpu.VMEM
    return pl.pallas_call(
        kernel,
        out_shape=jax.ShapeDtypeStruct((128, 128), F32),
        in_specs=[pl.BlockSpec(memory_space=pl.ANY)] * 2,
        out_specs=pl.BlockSpec(memory_space=pltpu.VMEM),
        scratch_shapes=[
            vmem((16, 512, 512), BF16),
            vmem((2 * COLS, 4096), BF16),
            vmem((2 * COLS, 512), F32),
            vmem((2 * COLS, 512), BF16),
            vmem((2, COLS, 512), BF16),
            vmem((2, 2 * COLS, 512), BF16),
            vmem((8, COLS, 512), F32),
            vmem((3, 4, COLS, 512), F32),
            vmem((3, 4, COLS, 512), F32),
            vmem((3, 8, COLS, 512), F32),
            vmem((8, COLS, 512), F32),
            vmem((8, COLS, 512), F32),
            vmem((2, 2 * COLS, 512), F32),
            vmem((2, 2, COLS, 512), F32),
            vmem((COLS, 128), F32),
            vmem((8, 1, 128), F32),
            vmem((4, COLS, 128), F32),
            vmem((4, COLS, 128), F32),
            vmem((8, COLS, 512), BF16),
            vmem((4, COLS, 512), BF16),
            vmem((8, COLS, 512), BF16),
            dma((2,)),
            dma((2, NP + 1, 8)),
            dma((2, NP + 1, 8)),
            dma((2, 16)),
            dma((2, 16)),
            dma((2, 16)),
            dma((2, 16)),
            dma((3,)),
            dma((3,)),
            dma((2,)),
            dma((2,)),
            dma((3, 4)),
            dma((3, 4)),
            dma((3, 4, CUTS)),
            dma((3, 4, CUTS)),
            dma((3, 4, CUTS)),
            dma((3, 4, CUTS)),
            dma((3, 4)),
            dma((3, 4)),
            dma((8,)),
            dma((8,)),
            dma((4,)),
            dma((4,)),
        ],
        compiler_params=pltpu.CompilerParams(
            collective_id=0, has_side_effects=True, vmem_limit_bytes=53 * 1024 * 1024 + 512 * 1024
        ),
    )(activations, jnp.swapaxes(weights, 1, 2))


def solution(mesh):
    in_specs = (P("mp", None, "row"), P("mp", None, ("row", "col")))
    out_specs = P(("row", "col"), "mp")
    return jax.shard_map(local, mesh=mesh, in_specs=in_specs, out_specs=out_specs, check_vma=False)
```

```python
import jax
import jax.numpy as jnp
from jax import lax
from jax.experimental import pallas as pl
from jax.experimental.pallas import tpu as pltpu
from jax.sharding import PartitionSpec as P

MESH = pl.DeviceIdType.MESH
F32 = jnp.float32
BF16 = jnp.bfloat16
NZ = (96, 80)
NP = len(NZ)
ZS = sum(NZ)
HALF = 176
COLS = 32
CUTS = 2


def fold(v):
    return v[:, :128] + v[:, 128:256] + v[:, 256:384] + v[:, 384:]


def total_of(v):
    return jnp.sum(v, axis=1, keepdims=True)


def kernel(
    a_hbm, w_hbm, out_ref,
    abuf, wbuf, yacc, yown, ycat, thl, ubuf, cbuf, rbuf, img, res, dir1, vacc, tok, dots, curv, mblk, obuf, narrow_parts, narrow_theirs, narrow_whole,
    in_sem, zs, zr, xs, xr, fs, fr, es, er, ys, yr, cs, cr, us, ur, gs, gr, hs, hr, ks, kr, os, orr,
):
    mp = lax.axis_index("mp")
    zl = lax.axis_index("row")
    x = lax.axis_index("col")
    y = lax.div(mp, 4)
    zh = lax.rem(lax.div(mp, 2), 2)
    k = lax.rem(mp, 2)
    z = 8 * zh + zl
    me = 2 * y + k

    def dev(dx, dy, dz, dk):
        return (4 * dy + 2 * lax.div(dz, 8) + dk, lax.rem(dz, 8), dx)

    def remote(src, dst, send, recv, device):
        return pltpu.make_async_remote_copy(
            src_ref=src, dst_ref=dst, send_sem=send, recv_sem=recv, device_id=device, device_id_type=MESH
        )

    def at_z(d):
        return lax.rem(z + d + 16, 16)

    def at_x(d):
        return lax.rem(x + d + 4, 4)

    def at_y(d):
        return lax.rem(y + d, 4)

    def member(b):
        return (4 * lax.div(b, 2) + 2 * zh + lax.rem(b, 2), zl, x)

    in_a = pltpu.make_async_copy(a_hbm.at[0], abuf.at[z], in_sem.at[0])
    in_w = pltpu.make_async_copy(w_hbm.at[0], wbuf, in_sem.at[1])
    in_a.start()
    in_w.start()

    barrier = pltpu.get_barrier_semaphore()

    def greet(device):
        pl.semaphore_signal(barrier, inc=1, device_id=device, device_id_type=MESH)

    greet(dev(x, y, at_z(1), k))
    greet(dev(x, y, at_z(-1), k))
    greet(dev(at_x(1), y, z, k))
    greet(dev(at_x(-1), y, z, k))

    @pl.loop(1, 8)
    def _(j):
        greet(member(lax.rem(me + j, 8)))

    in_a.wait()
    pl.semaphore_wait(barrier, 11)

    def piece(b, part, shard):
        if part < NP:
            return abuf.at[b, pl.ds(sum(NZ[:part]), NZ[part])]
        return abuf.at[b, pl.ds(ZS, 512 - ZS), pl.ds(pl.multiple_of(128 * shard, 128), 128)]

    def half_piece(b, d, shard):
        rows = pl.ds(ZS, HALF) if d == 0 else pl.ds(ZS + HALF, 512 - ZS - HALF)
        return abuf.at[b, rows, pl.ds(pl.multiple_of(128 * shard, 128), 128)]

    def steps(d, part):
        return 8 if (part < NP) == (d == 0) else 7

    def zlink(d, part, s, distance):
        sign = 1 - 2 * d
        ref = piece(at_z(-sign * distance), part, x)
        return remote(ref, ref, zs.at[d, part, s], zr.at[d, part, s], dev(x, y, at_z(sign), k))

    def zcopy(d, part, s):
        return zlink(d, part, s, s)

    def zrecv(d, part, s):
        return zlink(d, part, s, s + 1)

    def xcopy(d, b):
        ref = piece(b, NP, x)
        return remote(ref, ref, xs.at[d, b], xr.at[d, b], dev(at_x(1 - 2 * d), y, z, k))

    def xrecv(d, b):
        ref = piece(b, NP, at_x(2 * d - 1))
        return remote(ref, ref, xs.at[d, b], xr.at[d, b], dev(at_x(1 - 2 * d), y, z, k))

    def fcopy(d, b):
        ref = half_piece(b, d, at_x(2 * d - 1))
        return remote(ref, ref, fs.at[d, b], fr.at[d, b], dev(at_x(1 - 2 * d), y, z, k))

    def frecv(d, b):
        ref = half_piece(b, d, at_x(2))
        return remote(ref, ref, fs.at[d, b], fr.at[d, b], dev(at_x(1 - 2 * d), y, z, k))

    def finish(i, b):
        ref = piece(b, NP, at_x((1, -1, 2)[i]))
        return remote(ref, ref, es.at[i], er.at[i], dev(x, y, at_z(1 if i == 0 else -1), k))

    def pass_on(b):
        for d in range(2):
            xrecv(d, b).wait_recv()
            fcopy(d, b).start()

    def project(b):
        w = wbuf[:, pl.ds(pl.multiple_of(512 * lax.rem(b, 8), 512), 512)]
        yacc[...] += lax.dot_general(w, abuf[b], (((1,), (1,)), ((), ())), preferred_element_type=F32)

    def settle(b):
        for d in range(2):
            frecv(d, b).wait_recv()

        @pl.when(lax.div(b, 8) == zh)
        def _():
            project(b)

    for part in (NP, *range(NP)):
        for d in range(2):
            zcopy(d, part, 0).start()
    in_w.wait()
    yacc[...] = jnp.zeros_like(yacc)
    project(z)

    @pl.loop(1, 8)
    def _(s):
        def forward(part):
            for d in range(2):
                zrecv(d, part, s - 1).wait_recv()
                if steps(d, part) == 8:
                    zcopy(d, part, s).start()
                else:

                    @pl.when(s <= 6)
                    def _():
                        zcopy(d, part, s).start()

                if part == NP:
                    for e in range(2):
                        xcopy(e, at_z((2 * d - 1) * s)).start()

        forward(NP)

        @pl.when(s >= 2)
        def _():
            pass_on(at_z(1 - s))
            pass_on(at_z(s - 1))

        for part in range(NP):
            forward(part)

        @pl.when(s >= 3)
        def _():
            settle(at_z(2 - s))
            settle(at_z(s - 2))

    pass_on(at_z(7))
    finish(1, at_z(7)).start()
    pass_on(at_z(-7))
    finish(0, at_z(-7)).start()
    for d in (6, -6, 7):
        settle(at_z(d))
    finish(2, at_z(7)).start()
    settle(at_z(-7))

    yown[...] = yacc[...].astype(BF16)

    def ycopy(i):
        to = at_z(4 - 8 * i)
        away = yown.at[pl.ds(pl.multiple_of(COLS * lax.div(to, 8), COLS), COLS)]
        return remote(away, ycat.at[zh], ys.at[i], yr.at[i], dev(x, y, to, k))

    def yrecv(i):
        h = lax.div(at_z(8 * i - 4), 8)
        return remote(yown.at[pl.ds(0, COLS)], ycat.at[h], ys.at[i], yr.at[i], dev(x, y, at_z(4 - 8 * i), k))

    ycopy(0).start()
    ycopy(1).start()

    for part in range(NP):
        zrecv(0, part, 7).wait_recv()
    zrecv(1, NP, 7).wait_recv()
    for i in range(3):
        finish(i, at_z(8)).wait_recv()

    def gather_sent():
        for i in range(3):
            finish(i, at_z(-7 if i == 0 else 7)).wait_send()
        for i in range(2):
            ycopy(i).wait_send()

        @pl.loop(1, 8)
        def _(j):
            for d in range(2):
                for b in (at_z(j), at_z(-j)):
                    xcopy(d, b).wait_send()
                    fcopy(d, b).wait_send()

        for d in range(2):
            for part in range(NP + 1):

                @pl.loop(0, steps(d, part))
                def _(s):
                    zcopy(d, part, s).wait_send()

    for i in range(2):
        yrecv(i).wait_recv()

    sibling = dev(x, y, z, 1 - k)

    def all_reduce(rnd, block, arrive, meanwhile=None):
        narrow = rnd == 2
        cuts = 1 if narrow else CUTS
        mine = ubuf.at[rnd]
        parts = narrow_parts if narrow else mine
        theirs = narrow_theirs if narrow else rbuf.at[rnd]
        whole = narrow_whole if narrow else img.at[rnd]

        def core_part(o):
            q = at_y(o)
            return remote(mine.at[2 * q + 1 - k], cbuf.at[rnd, q], cs.at[rnd, q], cr.at[rnd, q], sibling)

        def cut(c):
            return pl.ds(c * (COLS // cuts), COLS // cuts)

        def ring_part(o, c):
            q = at_y(o)
            src, dst = parts.at[2 * q + k, cut(c)], theirs.at[y, cut(c)]
            return remote(src, dst, us.at[rnd, q, c], ur.at[rnd, y, c], dev(x, q, z, k))

        def ring_part_from(o, c):
            q = at_y(o)
            src, dst = parts.at[2 * q + k, cut(c)], theirs.at[q, cut(c)]
            return remote(src, dst, us.at[rnd, q, c], ur.at[rnd, q, c], dev(x, q, z, k))

        def ring_whole(o, c):
            q = at_y(o)
            ref = whole.at[me, cut(c)]
            return remote(ref, ref, gs.at[rnd, q, c], gr.at[rnd, y, c], dev(x, q, z, k))

        def ring_whole_from(o, c):
            q = at_y(o)
            ref = whole.at[2 * q + k, cut(c)]
            return remote(ref, ref, gs.at[rnd, q, c], gr.at[rnd, q, c], dev(x, q, z, k))

        def core_whole(o):
            q = at_y(o)
            ref = whole.at[2 * q + k]
            return remote(ref, ref, hs.at[rnd, q], hr.at[rnd, q], sibling)

        def core_whole_from(o):
            q = at_y(o)
            ref = whole.at[2 * q + 1 - k]
            return remote(ref, ref, hs.at[rnd, q], hr.at[rnd, q], sibling)

        def give(o):
            b = 2 * at_y(o) + 1 - k
            mine[b] = block(b)
            core_part(o).start()

        def keep(o):
            q = at_y(o)
            b = 2 * q + k
            own = block(b)
            remote(mine.at[b], cbuf.at[rnd, q], cs.at[rnd, q], cr.at[rnd, q], sibling).wait_recv()
            if o:
                parts[b] = (own + cbuf[rnd, q]).astype(parts.dtype)
                ring_part(o, 0).start()
            else:
                img[rnd, me] = own + cbuf[rnd, q]

        def widened(b):
            if narrow:
                img[rnd, b] = whole[b].astype(F32)
            arrive(b)

        give(2)
        give(1)
        keep(2)
        give(3)
        keep(1)
        give(0)
        keep(3)
        for c in range(1, cuts):
            for o in (2, 1, 3):
                ring_part(o, c).start()
        keep(0)
        if meanwhile:
            meanwhile()
        for c in range(cuts):
            for o in (1, 3, 2):
                ring_part_from(o, c).wait_recv()
            total = img[rnd, me, cut(c)] + (
                theirs[at_y(1), cut(c)].astype(F32)
                + theirs[at_y(3), cut(c)].astype(F32)
                + theirs[at_y(2), cut(c)].astype(F32)
            )
            whole[me, cut(c)] = total.astype(whole.dtype)
            for o in (2, 1, 3):
                ring_whole(o, c).start()
        core_whole(0).start()
        widened(me)
        core_whole_from(0).wait_recv()
        widened(2 * y + 1 - k)
        for o in (1, 3, 2):
            for c in range(cuts):
                ring_whole_from(o, c).wait_recv()
            core_whole(o).start()
            widened(2 * at_y(o) + k)
        for o in (1, 3, 2):
            core_whole_from(o).wait_recv()
            widened(2 * at_y(o) + 1 - k)

        def sent():
            for o in range(4):
                core_part(o).wait_send()
                core_whole(o).wait_send()
                if o:
                    for c in range(cuts):
                        ring_part(o, c).wait_send()
                        ring_whole(o, c).wait_send()

        return sent

    def split(v):
        hi = v.astype(BF16)
        return hi, (v - hi.astype(F32)).astype(BF16)

    def tokens_times(v, b):
        both = jnp.concatenate(split(v), axis=0)
        for h in range(2):
            vacc[h] += lax.dot_general(
                both, abuf[8 * h + b], (((1,), (1,)), ((), ())), preferred_element_type=F32
            )

    def products(h):
        return vacc[h, :COLS] + vacc[h, COLS:]

    def set_tokens(h, v):
        hi, lo = split(v)
        thl[h, pl.ds(0, COLS)] = hi
        thl[h, pl.ds(COLS, COLS)] = lo

    def rhs_block(b):
        return jnp.dot(ycat[0], abuf[b], preferred_element_type=F32) + jnp.dot(
            ycat[1], abuf[8 + b], preferred_element_type=F32
        )

    def image_block(b):
        both = jnp.dot(thl[0], abuf[b], preferred_element_type=F32) + jnp.dot(
            thl[1], abuf[8 + b], preferred_element_type=F32
        )
        return both[:COLS] + both[COLS:]

    def column_sum(term):
        acc = jnp.zeros((COLS, 128), F32)
        for b in range(8):
            acc = acc + fold(term(b))
        return total_of(acc)

    def arrived(rnd, direction):
        dots[...] = jnp.zeros_like(dots)

        def go(b):
            v = img[rnd, b]
            tokens_times(v, b)
            dots[...] += fold(v * direction(b))

        return go

    vacc[...] = jnp.zeros_like(vacc)
    sent0 = all_reduce(0, rhs_block, arrived(0, lambda b: img[0, b]))
    norm = total_of(dots[...])
    for h in range(2):
        t = products(h)
        set_tokens(h, t)
        tok[0, h] = t
        tok[1, h] = t
    vacc[...] = jnp.zeros_like(vacc)
    sent1 = all_reduce(1, image_block, arrived(1, lambda b: img[0, b]))
    alpha0 = norm / total_of(dots[...])
    for b in range(8):
        res[b] = img[0, b] - alpha0 * img[1, b]
    norm1 = column_sum(lambda b: res[b] * res[b])
    beta0 = norm1 / norm
    for h in range(2):
        t = tok[1, h] - alpha0 * products(h)
        tok[1, h] = t
        t = t + beta0 * tok[0, h]
        tok[0, h] = t
        set_tokens(h, t)

    def step_direction():
        for b in range(8):
            dir1[b] = res[b] + beta0 * img[0, b]

    vacc[...] = jnp.zeros_like(vacc)
    sent2 = all_reduce(2, image_block, arrived(2, lambda b: dir1[b]), step_direction)
    alpha1 = norm1 / total_of(dots[...])
    for b in range(8):
        res[b] = res[b] - alpha1 * img[2, b]
    norm2 = column_sum(lambda b: res[b] * res[b])
    beta = norm2 / norm1
    square = jnp.zeros((COLS, 128), F32)
    for h in range(2):
        t = tok[1, h] - alpha1 * products(h) + beta * tok[0, h]
        square = square + fold(t * t)
    diagonal = lax.broadcasted_iota(jnp.int32, (COLS, 128), 0) == lax.broadcasted_iota(jnp.int32, (COLS, 128), 1)
    curv[me] = jnp.sum(jnp.where(diagonal, total_of(square), 0.0), axis=0, keepdims=True)

    def kcopy(b):
        return remote(curv.at[me], curv.at[me], ks.at[b], kr.at[me], member(b))

    def krecv(b):
        return remote(curv.at[b], curv.at[b], ks.at[b], kr.at[b], member(b))

    @pl.loop(1, 8)
    def _(j):
        kcopy(lax.rem(me + j, 8)).start()

    known = alpha0 * img[0, me] + alpha1 * dir1[me]
    last = res[me] + beta * dir1[me]

    @pl.loop(1, 8)
    def _(j):
        krecv(lax.rem(me + j, 8)).wait_recv()

    curvature = curv[0]
    for b in range(1, 8):
        curvature = curvature + curv[b]
    alpha2 = norm2 / total_of(jnp.where(diagonal, curvature, 0.0))
    merged = known + alpha2 * last

    origin = lax.rem(zl + 4, 8)
    to_y, to_z, to_k = lax.div(origin, 2), 8 * lax.rem(origin, 2) + me, lax.div(x, 2)
    from_y, from_k = lax.div(zl, 2), lax.rem(zl, 2)
    slot = 2 * lax.rem(x, 2) + zh

    def out_self(dx):
        return (dx == x) & (to_y == y) & (to_z == z) & (to_k == k)

    def ocopy(dx):
        return remote(mblk.at[dx], obuf.at[slot], os.at[dx], orr.at[slot], dev(dx, to_y, to_z, to_k))

    for dx in range(4):
        mblk[dx] = merged[:, 128 * dx : 128 * (dx + 1)]

        @pl.when(jnp.logical_not(out_self(dx)))
        def _():
            ocopy(dx).start()

        @pl.when(out_self(dx))
        def _():
            obuf[slot] = mblk[dx]

    gather_sent()
    for sent in (sent0, sent1, sent2):
        sent()

    @pl.loop(1, 8)
    def _(j):
        kcopy(lax.rem(me + j, 8)).wait_send()

    for i in range(2):
        for h in range(2):
            q = 2 * i + h
            sx, sz = 2 * k + i, 8 * h + lax.rem(2 * y + zh + 4, 8)
            mine = (sx == x) & (from_y == y) & (sz == z) & (from_k == k)

            @pl.when(jnp.logical_not(mine))
            def _():
                remote(mblk.at[0], obuf.at[q], os.at[0], orr.at[q], dev(sx, from_y, sz, from_k)).wait_recv()

    for dx in range(4):

        @pl.when(jnp.logical_not(out_self(dx)))
        def _():
            ocopy(dx).wait_send()

    for q in range(4):
        out_ref[:, COLS * q : COLS * (q + 1)] = obuf[q].T


def local(activations, weights):
    dma = pltpu.SemaphoreType.DMA
    vmem = pltpu.VMEM
    return pl.pallas_call(
        kernel,
        out_shape=jax.ShapeDtypeStruct((128, 128), F32),
        in_specs=[pl.BlockSpec(memory_space=pl.ANY)] * 2,
        out_specs=pl.BlockSpec(memory_space=pltpu.VMEM),
        scratch_shapes=[
            vmem((16, 512, 512), BF16),
            vmem((2 * COLS, 4096), BF16),
            vmem((2 * COLS, 512), F32),
            vmem((2 * COLS, 512), BF16),
            vmem((2, COLS, 512), BF16),
            vmem((2, 2 * COLS, 512), BF16),
            vmem((3, 8, COLS, 512), F32),
            vmem((3, 4, COLS, 512), F32),
            vmem((3, 4, COLS, 512), F32),
            vmem((3, 8, COLS, 512), F32),
            vmem((8, COLS, 512), F32),
            vmem((8, COLS, 512), F32),
            vmem((2, 2 * COLS, 512), F32),
            vmem((2, 2, COLS, 512), F32),
            vmem((COLS, 128), F32),
            vmem((8, 1, 128), F32),
            vmem((4, COLS, 128), F32),
            vmem((4, COLS, 128), F32),
            vmem((8, COLS, 512), BF16),
            vmem((4, COLS, 512), BF16),
            vmem((8, COLS, 512), BF16),
            dma((2,)),
            dma((2, NP + 1, 8)),
            dma((2, NP + 1, 8)),
            dma((2, 16)),
            dma((2, 16)),
            dma((2, 16)),
            dma((2, 16)),
            dma((3,)),
            dma((3,)),
            dma((2,)),
            dma((2,)),
            dma((3, 4)),
            dma((3, 4)),
            dma((3, 4, CUTS)),
            dma((3, 4, CUTS)),
            dma((3, 4, CUTS)),
            dma((3, 4, CUTS)),
            dma((3, 4)),
            dma((3, 4)),
            dma((8,)),
            dma((8,)),
            dma((4,)),
            dma((4,)),
        ],
        compiler_params=pltpu.CompilerParams(
            collective_id=0, has_side_effects=True, vmem_limit_bytes=53 * 1024 * 1024 + 512 * 1024
        ),
    )(activations, jnp.swapaxes(weights, 1, 2))


def solution(mesh):
    in_specs = (P("mp", None, "row"), P("mp", None, ("row", "col")))
    out_specs = P(("row", "col"), "mp")
    return jax.shard_map(local, mesh=mesh, in_specs=in_specs, out_specs=out_specs, check_vma=False)
```

```python
import jax
import jax.numpy as jnp
from jax import lax
from jax.experimental import pallas as pl
from jax.experimental.pallas import tpu as pltpu
from jax.sharding import PartitionSpec as P

MESH = pl.DeviceIdType.MESH
F32 = jnp.float32
BF16 = jnp.bfloat16
NZ = (96, 80)
NP = len(NZ)
ZS = sum(NZ)
HALF = 176
COLS = 32
CUTS = 2


def fold(v):
    return v[:, :128] + v[:, 128:256] + v[:, 256:384] + v[:, 384:]


def total_of(v):
    return jnp.sum(v, axis=1, keepdims=True)


def kernel(
    a_hbm, w_hbm, out_ref,
    abuf, wbuf, yacc, yown, ycat, thl, ubuf, cbuf, rbuf, img, res, dir1, vacc, tok, dots, curv, mblk, obuf, narrow_parts, narrow_theirs, narrow_whole,
    in_sem, zs, zr, xs, xr, fs, fr, es, er, ys, yr, cs, cr, us, ur, gs, gr, hs, hr, ks, kr, os, orr,
):
    mp = lax.axis_index("mp")
    zl = lax.axis_index("row")
    x = lax.axis_index("col")
    y = lax.div(mp, 4)
    zh = lax.rem(lax.div(mp, 2), 2)
    k = lax.rem(mp, 2)
    z = 8 * zh + zl
    me = 2 * y + k

    def dev(dx, dy, dz, dk):
        return (4 * dy + 2 * lax.div(dz, 8) + dk, lax.rem(dz, 8), dx)

    def remote(src, dst, send, recv, device):
        return pltpu.make_async_remote_copy(
            src_ref=src, dst_ref=dst, send_sem=send, recv_sem=recv, device_id=device, device_id_type=MESH
        )

    def at_z(d):
        return lax.rem(z + d + 16, 16)

    def at_x(d):
        return lax.rem(x + d + 4, 4)

    def at_y(d):
        return lax.rem(y + d, 4)

    def member(b):
        return (4 * lax.div(b, 2) + 2 * zh + lax.rem(b, 2), zl, x)

    in_a = pltpu.make_async_copy(a_hbm.at[0], abuf.at[z], in_sem.at[0])
    in_w = pltpu.make_async_copy(w_hbm.at[0], wbuf, in_sem.at[1])
    in_a.start()
    in_w.start()

    barrier = pltpu.get_barrier_semaphore()

    def greet(device):
        pl.semaphore_signal(barrier, inc=1, device_id=device, device_id_type=MESH)

    greet(dev(x, y, at_z(1), k))
    greet(dev(x, y, at_z(-1), k))
    greet(dev(at_x(1), y, z, k))
    greet(dev(at_x(-1), y, z, k))

    @pl.loop(1, 8)
    def _(j):
        greet(member(lax.rem(me + j, 8)))

    in_a.wait()
    pl.semaphore_wait(barrier, 11)

    def piece(b, part, shard):
        if part < NP:
            return abuf.at[b, pl.ds(sum(NZ[:part]), NZ[part])]
        return abuf.at[b, pl.ds(ZS, 512 - ZS), pl.ds(pl.multiple_of(128 * shard, 128), 128)]

    def half_piece(b, d, shard):
        rows = pl.ds(ZS, HALF) if d == 0 else pl.ds(ZS + HALF, 512 - ZS - HALF)
        return abuf.at[b, rows, pl.ds(pl.multiple_of(128 * shard, 128), 128)]

    def steps(d, part):
        return 8 if (part < NP) == (d == 0) else 7

    def zlink(d, part, s, distance):
        sign = 1 - 2 * d
        ref = piece(at_z(-sign * distance), part, x)
        return remote(ref, ref, zs.at[d, part, s], zr.at[d, part, s], dev(x, y, at_z(sign), k))

    def zcopy(d, part, s):
        return zlink(d, part, s, s)

    def zrecv(d, part, s):
        return zlink(d, part, s, s + 1)

    def xcopy(d, b):
        ref = piece(b, NP, x)
        return remote(ref, ref, xs.at[d, b], xr.at[d, b], dev(at_x(1 - 2 * d), y, z, k))

    def xrecv(d, b):
        ref = piece(b, NP, at_x(2 * d - 1))
        return remote(ref, ref, xs.at[d, b], xr.at[d, b], dev(at_x(1 - 2 * d), y, z, k))

    def fcopy(d, b):
        ref = half_piece(b, d, at_x(2 * d - 1))
        return remote(ref, ref, fs.at[d, b], fr.at[d, b], dev(at_x(1 - 2 * d), y, z, k))

    def frecv(d, b):
        ref = half_piece(b, d, at_x(2))
        return remote(ref, ref, fs.at[d, b], fr.at[d, b], dev(at_x(1 - 2 * d), y, z, k))

    def finish(i, b):
        ref = piece(b, NP, at_x((1, -1, 2)[i]))
        return remote(ref, ref, es.at[i], er.at[i], dev(x, y, at_z(1 if i == 0 else -1), k))

    def pass_on(b):
        for d in range(2):
            xrecv(d, b).wait_recv()
            fcopy(d, b).start()

    def project(b):
        w = wbuf[:, pl.ds(pl.multiple_of(512 * lax.rem(b, 8), 512), 512)]
        yacc[...] += lax.dot_general(w, abuf[b], (((1,), (1,)), ((), ())), preferred_element_type=F32)

    def settle(b):
        for d in range(2):
            frecv(d, b).wait_recv()

        @pl.when(lax.div(b, 8) == zh)
        def _():
            project(b)

    for part in (NP, *range(NP)):
        for d in range(2):
            zcopy(d, part, 0).start()
    in_w.wait()
    yacc[...] = jnp.zeros_like(yacc)
    project(z)

    @pl.loop(1, 8)
    def _(s):
        def forward(part):
            for d in range(2):
                zrecv(d, part, s - 1).wait_recv()
                if steps(d, part) == 8:
                    zcopy(d, part, s).start()
                else:

                    @pl.when(s <= 6)
                    def _():
                        zcopy(d, part, s).start()

                if part == NP:
                    for e in range(2):
                        xcopy(e, at_z((2 * d - 1) * s)).start()

        forward(NP)

        @pl.when(s >= 2)
        def _():
            pass_on(at_z(1 - s))
            pass_on(at_z(s - 1))

        for part in range(NP):
            forward(part)

        @pl.when(s >= 3)
        def _():
            settle(at_z(2 - s))
            settle(at_z(s - 2))

    pass_on(at_z(7))
    finish(1, at_z(7)).start()
    pass_on(at_z(-7))
    finish(0, at_z(-7)).start()
    for d in (6, -6, 7):
        settle(at_z(d))
    finish(2, at_z(7)).start()
    settle(at_z(-7))

    yown[...] = yacc[...].astype(BF16)

    def ycopy(i):
        to = at_z(4 - 8 * i)
        away = yown.at[pl.ds(pl.multiple_of(COLS * lax.div(to, 8), COLS), COLS)]
        return remote(away, ycat.at[zh], ys.at[i], yr.at[i], dev(x, y, to, k))

    def yrecv(i):
        h = lax.div(at_z(8 * i - 4), 8)
        return remote(yown.at[pl.ds(0, COLS)], ycat.at[h], ys.at[i], yr.at[i], dev(x, y, at_z(4 - 8 * i), k))

    ycopy(0).start()
    ycopy(1).start()

    for part in range(NP):
        zrecv(0, part, 7).wait_recv()
    zrecv(1, NP, 7).wait_recv()
    for i in range(3):
        finish(i, at_z(8)).wait_recv()

    def gather_sent():
        for i in range(3):
            finish(i, at_z(-7 if i == 0 else 7)).wait_send()
        for i in range(2):
            ycopy(i).wait_send()

        @pl.loop(1, 8)
        def _(j):
            for d in range(2):
                for b in (at_z(j), at_z(-j)):
                    xcopy(d, b).wait_send()
                    fcopy(d, b).wait_send()

        for d in range(2):
            for part in range(NP + 1):

                @pl.loop(0, steps(d, part))
                def _(s):
                    zcopy(d, part, s).wait_send()

    for i in range(2):
        yrecv(i).wait_recv()

    sibling = dev(x, y, z, 1 - k)

    def all_reduce(rnd, block, arrive, meanwhile=None):
        narrow = rnd == 2
        cuts = 1 if narrow else CUTS
        mine = ubuf.at[rnd]
        parts = narrow_parts if narrow else mine
        theirs = narrow_theirs if narrow else rbuf.at[rnd]
        whole = narrow_whole if narrow else img.at[rnd]

        def core_part(o):
            q = at_y(o)
            return remote(mine.at[2 * q + 1 - k], cbuf.at[rnd, q], cs.at[rnd, q], cr.at[rnd, q], sibling)

        def cut(c):
            return pl.ds(c * (COLS // cuts), COLS // cuts)

        def ring_part(o, c):
            q = at_y(o)
            src, dst = parts.at[2 * q + k, cut(c)], theirs.at[y, cut(c)]
            return remote(src, dst, us.at[rnd, q, c], ur.at[rnd, y, c], dev(x, q, z, k))

        def ring_part_from(o, c):
            q = at_y(o)
            src, dst = parts.at[2 * q + k, cut(c)], theirs.at[q, cut(c)]
            return remote(src, dst, us.at[rnd, q, c], ur.at[rnd, q, c], dev(x, q, z, k))

        def ring_whole(o, c):
            q = at_y(o)
            ref = whole.at[me, cut(c)]
            return remote(ref, ref, gs.at[rnd, q, c], gr.at[rnd, y, c], dev(x, q, z, k))

        def ring_whole_from(o, c):
            q = at_y(o)
            ref = whole.at[2 * q + k, cut(c)]
            return remote(ref, ref, gs.at[rnd, q, c], gr.at[rnd, q, c], dev(x, q, z, k))

        def core_whole(o):
            q = at_y(o)
            ref = whole.at[2 * q + k]
            return remote(ref, ref, hs.at[rnd, q], hr.at[rnd, q], sibling)

        def core_whole_from(o):
            q = at_y(o)
            ref = whole.at[2 * q + 1 - k]
            return remote(ref, ref, hs.at[rnd, q], hr.at[rnd, q], sibling)

        def give(o):
            b = 2 * at_y(o) + 1 - k
            mine[b] = block(b)
            core_part(o).start()

        def keep(o):
            q = at_y(o)
            b = 2 * q + k
            own = block(b)
            remote(mine.at[b], cbuf.at[rnd, q], cs.at[rnd, q], cr.at[rnd, q], sibling).wait_recv()
            if o:
                parts[b] = (own + cbuf[rnd, q]).astype(parts.dtype)
                ring_part(o, 0).start()
            else:
                img[rnd, me] = own + cbuf[rnd, q]

        def widened(b):
            if narrow:
                img[rnd, b] = whole[b].astype(F32)
            arrive(b)

        give(2)
        give(1)
        keep(2)
        give(3)
        keep(1)
        give(0)
        keep(3)
        for c in range(1, cuts):
            for o in (2, 1, 3):
                ring_part(o, c).start()
        keep(0)
        if meanwhile:
            meanwhile()
        for c in range(cuts):
            for o in (1, 3, 2):
                ring_part_from(o, c).wait_recv()
            total = img[rnd, me, cut(c)] + (
                theirs[at_y(1), cut(c)].astype(F32)
                + theirs[at_y(3), cut(c)].astype(F32)
                + theirs[at_y(2), cut(c)].astype(F32)
            )
            whole[me, cut(c)] = total.astype(whole.dtype)
            for o in (2, 1, 3):
                ring_whole(o, c).start()
        core_whole(0).start()
        widened(me)
        core_whole_from(0).wait_recv()
        widened(2 * y + 1 - k)
        for o in (1, 3, 2):
            for c in range(cuts):
                ring_whole_from(o, c).wait_recv()
            core_whole(o).start()
            widened(2 * at_y(o) + k)
        for o in (1, 3, 2):
            core_whole_from(o).wait_recv()
            widened(2 * at_y(o) + 1 - k)

        def sent():
            for o in range(4):
                core_part(o).wait_send()
                core_whole(o).wait_send()
                if o:
                    for c in range(cuts):
                        ring_part(o, c).wait_send()
                        ring_whole(o, c).wait_send()

        return sent

    def split(v):
        hi = v.astype(BF16)
        return hi, (v - hi.astype(F32)).astype(BF16)

    def tokens_times(v, b):
        both = jnp.concatenate(split(v), axis=0)
        for h in range(2):
            vacc[h] += lax.dot_general(
                both, abuf[8 * h + b], (((1,), (1,)), ((), ())), preferred_element_type=F32
            )

    def products(h):
        return vacc[h, :COLS] + vacc[h, COLS:]

    def set_tokens(h, v):
        hi, lo = split(v)
        thl[h, pl.ds(0, COLS)] = hi
        thl[h, pl.ds(COLS, COLS)] = lo

    def rhs_block(b):
        return jnp.dot(ycat[0], abuf[b], preferred_element_type=F32) + jnp.dot(
            ycat[1], abuf[8 + b], preferred_element_type=F32
        )

    def image_block(b):
        both = jnp.dot(thl[0], abuf[b], preferred_element_type=F32) + jnp.dot(
            thl[1], abuf[8 + b], preferred_element_type=F32
        )
        return both[:COLS] + both[COLS:]

    def column_sum(term):
        acc = jnp.zeros((COLS, 128), F32)
        for b in range(8):
            acc = acc + fold(term(b))
        return total_of(acc)

    def arrived(rnd, direction):
        dots[...] = jnp.zeros_like(dots)

        def go(b):
            v = img[rnd, b]
            tokens_times(v, b)
            dots[...] += fold(v * direction(b))

        return go

    vacc[...] = jnp.zeros_like(vacc)
    sent0 = all_reduce(0, rhs_block, arrived(0, lambda b: img[0, b]))
    norm = total_of(dots[...])
    for h in range(2):
        t = products(h)
        set_tokens(h, t)
        tok[0, h] = t
        tok[1, h] = t
    vacc[...] = jnp.zeros_like(vacc)
    sent1 = all_reduce(1, image_block, arrived(1, lambda b: img[0, b]))
    alpha0 = norm / total_of(dots[...])
    for b in range(8):
        res[b] = img[0, b] - alpha0 * img[1, b]
    norm1 = column_sum(lambda b: res[b] * res[b])
    beta0 = norm1 / norm
    for h in range(2):
        t = tok[1, h] - alpha0 * products(h)
        tok[1, h] = t
        t = t + beta0 * tok[0, h]
        tok[0, h] = t
        set_tokens(h, t)

    def step_direction():
        for b in range(8):
            dir1[b] = res[b] + beta0 * img[0, b]

    vacc[...] = jnp.zeros_like(vacc)
    sent2 = all_reduce(2, image_block, arrived(2, lambda b: dir1[b]), step_direction)
    alpha1 = norm1 / total_of(dots[...])
    for b in range(8):
        res[b] = res[b] - alpha1 * img[2, b]
    norm2 = column_sum(lambda b: res[b] * res[b])
    beta = norm2 / norm1
    square = jnp.zeros((COLS, 128), F32)
    for h in range(2):
        t = tok[1, h] - alpha1 * products(h) + beta * tok[0, h]
        square = square + fold(t * t)
    diagonal = lax.broadcasted_iota(jnp.int32, (COLS, 128), 0) == lax.broadcasted_iota(jnp.int32, (COLS, 128), 1)
    curv[me] = jnp.sum(jnp.where(diagonal, total_of(square), 0.0), axis=0, keepdims=True)

    def kcopy(b):
        return remote(curv.at[me], curv.at[me], ks.at[b], kr.at[me], member(b))

    def krecv(b):
        return remote(curv.at[b], curv.at[b], ks.at[b], kr.at[b], member(b))

    @pl.loop(1, 8)
    def _(j):
        kcopy(lax.rem(me + j, 8)).start()

    def sent_block(dx):
        return lax.rem(me + 2 * dx, 8)

    known, last = [], []
    for dx in range(4):
        b, lanes = sent_block(dx), pl.ds(128 * dx, 128)
        known.append(alpha0 * img[0, b, :, lanes] + alpha1 * dir1[b, :, lanes])
        last.append(res[b, :, lanes] + beta * dir1[b, :, lanes])

    @pl.loop(1, 8)
    def _(j):
        krecv(lax.rem(me + j, 8)).wait_recv()

    curvature = curv[0]
    for b in range(1, 8):
        curvature = curvature + curv[b]
    alpha2 = norm2 / total_of(jnp.where(diagonal, curvature, 0.0))

    origin = lax.rem(zl + 4, 8)
    to_y, to_k = lax.div(origin, 2), lax.div(x, 2)
    sender = lax.rem(zl + 8 - 2 * x, 8)
    from_y, from_k = lax.div(sender, 2), lax.rem(sender, 2)
    slot = 2 * lax.rem(x, 2) + zh

    def to_z(dx):
        return 8 * lax.rem(origin, 2) + sent_block(dx)

    def out_self(dx):
        return (dx == x) & (to_y == y) & (to_z(dx) == z) & (to_k == k)

    def ocopy(dx):
        return remote(mblk.at[dx], obuf.at[slot], os.at[dx], orr.at[slot], dev(dx, to_y, to_z(dx), to_k))

    for dx in range(4):
        mblk[dx] = known[dx] + alpha2 * last[dx]

        @pl.when(jnp.logical_not(out_self(dx)))
        def _():
            ocopy(dx).start()

        @pl.when(out_self(dx))
        def _():
            obuf[slot] = mblk[dx]

    gather_sent()
    for sent in (sent0, sent1, sent2):
        sent()

    @pl.loop(1, 8)
    def _(j):
        kcopy(lax.rem(me + j, 8)).wait_send()

    for i in range(2):
        for h in range(2):
            q = 2 * i + h
            sx, sz = 2 * k + i, 8 * h + lax.rem(2 * y + zh + 4, 8)
            mine = (sx == x) & (from_y == y) & (sz == z) & (from_k == k)

            @pl.when(jnp.logical_not(mine))
            def _():
                remote(mblk.at[0], obuf.at[q], os.at[0], orr.at[q], dev(sx, from_y, sz, from_k)).wait_recv()

    for dx in range(4):

        @pl.when(jnp.logical_not(out_self(dx)))
        def _():
            ocopy(dx).wait_send()

    for q in range(4):
        out_ref[:, COLS * q : COLS * (q + 1)] = obuf[q].T


def local(activations, weights):
    dma = pltpu.SemaphoreType.DMA
    vmem = pltpu.VMEM
    return pl.pallas_call(
        kernel,
        out_shape=jax.ShapeDtypeStruct((128, 128), F32),
        in_specs=[pl.BlockSpec(memory_space=pl.ANY)] * 2,
        out_specs=pl.BlockSpec(memory_space=pltpu.VMEM),
        scratch_shapes=[
            vmem((16, 512, 512), BF16),
            vmem((2 * COLS, 4096), BF16),
            vmem((2 * COLS, 512), F32),
            vmem((2 * COLS, 512), BF16),
            vmem((2, COLS, 512), BF16),
            vmem((2, 2 * COLS, 512), BF16),
            vmem((3, 8, COLS, 512), F32),
            vmem((3, 4, COLS, 512), F32),
            vmem((3, 4, COLS, 512), F32),
            vmem((3, 8, COLS, 512), F32),
            vmem((8, COLS, 512), F32),
            vmem((8, COLS, 512), F32),
            vmem((2, 2 * COLS, 512), F32),
            vmem((2, 2, COLS, 512), F32),
            vmem((COLS, 128), F32),
            vmem((8, 1, 128), F32),
            vmem((4, COLS, 128), F32),
            vmem((4, COLS, 128), F32),
            vmem((8, COLS, 512), BF16),
            vmem((4, COLS, 512), BF16),
            vmem((8, COLS, 512), BF16),
            dma((2,)),
            dma((2, NP + 1, 8)),
            dma((2, NP + 1, 8)),
            dma((2, 16)),
            dma((2, 16)),
            dma((2, 16)),
            dma((2, 16)),
            dma((3,)),
            dma((3,)),
            dma((2,)),
            dma((2,)),
            dma((3, 4)),
            dma((3, 4)),
            dma((3, 4, CUTS)),
            dma((3, 4, CUTS)),
            dma((3, 4, CUTS)),
            dma((3, 4, CUTS)),
            dma((3, 4)),
            dma((3, 4)),
            dma((8,)),
            dma((8,)),
            dma((4,)),
            dma((4,)),
        ],
        compiler_params=pltpu.CompilerParams(
            collective_id=0, has_side_effects=True, vmem_limit_bytes=53 * 1024 * 1024 + 512 * 1024
        ),
    )(activations, jnp.swapaxes(weights, 1, 2))


def solution(mesh):
    in_specs = (P("mp", None, "row"), P("mp", None, ("row", "col")))
    out_specs = P(("row", "col"), "mp")
    return jax.shard_map(local, mesh=mesh, in_specs=in_specs, out_specs=out_specs, check_vma=False)
```

```python
import jax
import jax.numpy as jnp
from jax import lax
from jax.experimental import pallas as pl
from jax.experimental.pallas import tpu as pltpu
from jax.sharding import PartitionSpec as P

MESH = pl.DeviceIdType.MESH
F32 = jnp.float32
BF16 = jnp.bfloat16
NZ = (96, 80)
NP = len(NZ)
ZS = sum(NZ)
HALF = 176
COLS = 32
CUTS = 2


def fold(v):
    return v[:, :128] + v[:, 128:256] + v[:, 256:384] + v[:, 384:]


def total_of(v):
    return jnp.sum(v, axis=1, keepdims=True)


def kernel(
    a_hbm, w_hbm, out_ref,
    abuf, wbuf, yacc, yown, ycat, thl, ubuf, cbuf, rbuf, img, res, dir1, vacc, tok, dots, curv, mblk, obuf, narrow_parts, narrow_theirs, narrow_whole,
    in_sem, zs, zr, xs, xr, fs, fr, es, er, ys, yr, cs, cr, us, ur, gs, gr, hs, hr, ks, kr, os, orr,
):
    mp = lax.axis_index("mp")
    zl = lax.axis_index("row")
    x = lax.axis_index("col")
    y = lax.div(mp, 4)
    zh = lax.rem(lax.div(mp, 2), 2)
    k = lax.rem(mp, 2)
    z = 8 * zh + zl
    me = 2 * y + k

    def dev(dx, dy, dz, dk):
        return (4 * dy + 2 * lax.div(dz, 8) + dk, lax.rem(dz, 8), dx)

    def remote(src, dst, send, recv, device):
        return pltpu.make_async_remote_copy(
            src_ref=src, dst_ref=dst, send_sem=send, recv_sem=recv, device_id=device, device_id_type=MESH
        )

    def at_z(d):
        return lax.rem(z + d + 16, 16)

    def at_x(d):
        return lax.rem(x + d + 4, 4)

    def at_y(d):
        return lax.rem(y + d, 4)

    def member(b):
        return (4 * lax.div(b, 2) + 2 * zh + lax.rem(b, 2), zl, x)

    in_a = pltpu.make_async_copy(a_hbm.at[0], abuf.at[z], in_sem.at[0])
    in_w = pltpu.make_async_copy(w_hbm.at[0], wbuf, in_sem.at[1])
    in_a.start()
    in_w.start()

    barrier = pltpu.get_barrier_semaphore()

    def greet(device):
        pl.semaphore_signal(barrier, inc=1, device_id=device, device_id_type=MESH)

    greet(dev(x, y, at_z(1), k))
    greet(dev(x, y, at_z(-1), k))
    greet(dev(at_x(1), y, z, k))
    greet(dev(at_x(-1), y, z, k))

    @pl.loop(1, 8)
    def _(j):
        greet(member(lax.rem(me + j, 8)))

    in_a.wait()
    pl.semaphore_wait(barrier, 11)

    def piece(b, part, shard):
        if part < NP:
            return abuf.at[b, pl.ds(sum(NZ[:part]), NZ[part])]
        return abuf.at[b, pl.ds(ZS, 512 - ZS), pl.ds(pl.multiple_of(128 * shard, 128), 128)]

    def half_piece(b, d, shard):
        rows = pl.ds(ZS, HALF) if d == 0 else pl.ds(ZS + HALF, 512 - ZS - HALF)
        return abuf.at[b, rows, pl.ds(pl.multiple_of(128 * shard, 128), 128)]

    def steps(d, part):
        return 8 if (part < NP) == (d == 0) else 7

    def zlink(d, part, s, distance):
        sign = 1 - 2 * d
        ref = piece(at_z(-sign * distance), part, x)
        return remote(ref, ref, zs.at[d, part, s], zr.at[d, part, s], dev(x, y, at_z(sign), k))

    def zcopy(d, part, s):
        return zlink(d, part, s, s)

    def zrecv(d, part, s):
        return zlink(d, part, s, s + 1)

    def xcopy(d, b):
        ref = piece(b, NP, x)
        return remote(ref, ref, xs.at[d, b], xr.at[d, b], dev(at_x(1 - 2 * d), y, z, k))

    def xrecv(d, b):
        ref = piece(b, NP, at_x(2 * d - 1))
        return remote(ref, ref, xs.at[d, b], xr.at[d, b], dev(at_x(1 - 2 * d), y, z, k))

    def fcopy(d, b):
        ref = half_piece(b, d, at_x(2 * d - 1))
        return remote(ref, ref, fs.at[d, b], fr.at[d, b], dev(at_x(1 - 2 * d), y, z, k))

    def frecv(d, b):
        ref = half_piece(b, d, at_x(2))
        return remote(ref, ref, fs.at[d, b], fr.at[d, b], dev(at_x(1 - 2 * d), y, z, k))

    def finish(i, b):
        ref = piece(b, NP, at_x((1, -1, 2)[i]))
        return remote(ref, ref, es.at[i], er.at[i], dev(x, y, at_z(1 if i == 0 else -1), k))

    def pass_on(b):
        for d in range(2):
            xrecv(d, b).wait_recv()
            fcopy(d, b).start()

    def project(b):
        w = wbuf[:, pl.ds(pl.multiple_of(512 * lax.rem(b, 8), 512), 512)]
        yacc[...] += lax.dot_general(w, abuf[b], (((1,), (1,)), ((), ())), preferred_element_type=F32)

    def settle(b):
        for d in range(2):
            frecv(d, b).wait_recv()

        @pl.when(lax.div(b, 8) == zh)
        def _():
            project(b)

    for part in (NP, *range(NP)):
        for d in range(2):
            zcopy(d, part, 0).start()
    in_w.wait()
    yacc[...] = jnp.zeros_like(yacc)
    project(z)

    @pl.loop(1, 8)
    def _(s):
        def forward(part):
            for d in range(2):
                zrecv(d, part, s - 1).wait_recv()
                if steps(d, part) == 8:
                    zcopy(d, part, s).start()
                else:

                    @pl.when(s <= 6)
                    def _():
                        zcopy(d, part, s).start()

                if part == NP:
                    for e in range(2):
                        xcopy(e, at_z((2 * d - 1) * s)).start()

        forward(NP)

        @pl.when(s >= 2)
        def _():
            pass_on(at_z(1 - s))
            pass_on(at_z(s - 1))

        for part in range(NP):
            forward(part)

        @pl.when(s >= 3)
        def _():
            settle(at_z(2 - s))
            settle(at_z(s - 2))

    pass_on(at_z(7))
    finish(1, at_z(7)).start()
    pass_on(at_z(-7))
    finish(0, at_z(-7)).start()
    for d in (6, -6, 7, -7):
        settle(at_z(d))

    yown[...] = yacc[...].astype(BF16)

    def ycopy(i):
        to = at_z(4 - 8 * i)
        away = yown.at[pl.ds(pl.multiple_of(COLS * lax.div(to, 8), COLS), COLS)]
        return remote(away, ycat.at[zh], ys.at[i], yr.at[i], dev(x, y, to, k))

    def yrecv(i):
        h = lax.div(at_z(8 * i - 4), 8)
        return remote(yown.at[pl.ds(0, COLS)], ycat.at[h], ys.at[i], yr.at[i], dev(x, y, at_z(4 - 8 * i), k))

    ycopy(0).start()
    ycopy(1).start()
    finish(2, at_z(7)).start()

    for part in range(NP):
        zrecv(0, part, 7).wait_recv()
    zrecv(1, NP, 7).wait_recv()
    for i in range(3):
        finish(i, at_z(8)).wait_recv()

    def gather_sent():
        for i in range(3):
            finish(i, at_z(-7 if i == 0 else 7)).wait_send()
        for i in range(2):
            ycopy(i).wait_send()

        @pl.loop(1, 8)
        def _(j):
            for d in range(2):
                for b in (at_z(j), at_z(-j)):
                    xcopy(d, b).wait_send()
                    fcopy(d, b).wait_send()

        for d in range(2):
            for part in range(NP + 1):

                @pl.loop(0, steps(d, part))
                def _(s):
                    zcopy(d, part, s).wait_send()

    for i in range(2):
        yrecv(i).wait_recv()

    sibling = dev(x, y, z, 1 - k)

    def all_reduce(rnd, block, arrive, meanwhile=None):
        narrow = rnd == 2
        cuts = 1 if narrow else CUTS
        mine = ubuf.at[rnd]
        parts = narrow_parts if narrow else mine
        theirs = narrow_theirs if narrow else rbuf.at[rnd]
        whole = narrow_whole if narrow else img.at[rnd]

        def core_part(o):
            q = at_y(o)
            return remote(mine.at[2 * q + 1 - k], cbuf.at[rnd, q], cs.at[rnd, q], cr.at[rnd, q], sibling)

        def cut(c):
            return pl.ds(c * (COLS // cuts), COLS // cuts)

        def ring_part(o, c):
            q = at_y(o)
            src, dst = parts.at[2 * q + k, cut(c)], theirs.at[y, cut(c)]
            return remote(src, dst, us.at[rnd, q, c], ur.at[rnd, y, c], dev(x, q, z, k))

        def ring_part_from(o, c):
            q = at_y(o)
            src, dst = parts.at[2 * q + k, cut(c)], theirs.at[q, cut(c)]
            return remote(src, dst, us.at[rnd, q, c], ur.at[rnd, q, c], dev(x, q, z, k))

        def ring_whole(o, c):
            q = at_y(o)
            ref = whole.at[me, cut(c)]
            return remote(ref, ref, gs.at[rnd, q, c], gr.at[rnd, y, c], dev(x, q, z, k))

        def ring_whole_from(o, c):
            q = at_y(o)
            ref = whole.at[2 * q + k, cut(c)]
            return remote(ref, ref, gs.at[rnd, q, c], gr.at[rnd, q, c], dev(x, q, z, k))

        def core_whole(o):
            q = at_y(o)
            ref = whole.at[2 * q + k]
            return remote(ref, ref, hs.at[rnd, q], hr.at[rnd, q], sibling)

        def core_whole_from(o):
            q = at_y(o)
            ref = whole.at[2 * q + 1 - k]
            return remote(ref, ref, hs.at[rnd, q], hr.at[rnd, q], sibling)

        def give(o):
            b = 2 * at_y(o) + 1 - k
            mine[b] = block(b)
            core_part(o).start()

        def keep(o):
            q = at_y(o)
            b = 2 * q + k
            own = block(b)
            remote(mine.at[b], cbuf.at[rnd, q], cs.at[rnd, q], cr.at[rnd, q], sibling).wait_recv()
            if o:
                parts[b] = (own + cbuf[rnd, q]).astype(parts.dtype)
                ring_part(o, 0).start()
            else:
                img[rnd, me] = own + cbuf[rnd, q]

        def widened(b):
            if narrow:
                img[rnd, b] = whole[b].astype(F32)
            arrive(b)

        give(2)
        give(1)
        keep(2)
        give(3)
        keep(1)
        give(0)
        keep(3)
        for c in range(1, cuts):
            for o in (2, 1, 3):
                ring_part(o, c).start()
        keep(0)
        if meanwhile:
            meanwhile()
        for c in range(cuts):
            for o in (1, 3, 2):
                ring_part_from(o, c).wait_recv()
            total = img[rnd, me, cut(c)] + (
                theirs[at_y(1), cut(c)].astype(F32)
                + theirs[at_y(3), cut(c)].astype(F32)
                + theirs[at_y(2), cut(c)].astype(F32)
            )
            whole[me, cut(c)] = total.astype(whole.dtype)
            for o in (2, 1, 3):
                ring_whole(o, c).start()
        core_whole(0).start()
        widened(me)
        core_whole_from(0).wait_recv()
        widened(2 * y + 1 - k)
        for o in (1, 3, 2):
            for c in range(cuts):
                ring_whole_from(o, c).wait_recv()
            core_whole(o).start()
            widened(2 * at_y(o) + k)
        for o in (1, 3, 2):
            core_whole_from(o).wait_recv()
            widened(2 * at_y(o) + 1 - k)

        def sent():
            for o in range(4):
                core_part(o).wait_send()
                core_whole(o).wait_send()
                if o:
                    for c in range(cuts):
                        ring_part(o, c).wait_send()
                        ring_whole(o, c).wait_send()

        return sent

    def split(v):
        hi = v.astype(BF16)
        return hi, (v - hi.astype(F32)).astype(BF16)

    def tokens_times(v, b):
        both = jnp.concatenate(split(v), axis=0)
        for h in range(2):
            vacc[h] += lax.dot_general(
                both, abuf[8 * h + b], (((1,), (1,)), ((), ())), preferred_element_type=F32
            )

    def products(h):
        return vacc[h, :COLS] + vacc[h, COLS:]

    def set_tokens(h, v):
        hi, lo = split(v)
        thl[h, pl.ds(0, COLS)] = hi
        thl[h, pl.ds(COLS, COLS)] = lo

    def rhs_block(b):
        return jnp.dot(ycat[0], abuf[b], preferred_element_type=F32) + jnp.dot(
            ycat[1], abuf[8 + b], preferred_element_type=F32
        )

    def image_block(b):
        both = jnp.dot(thl[0], abuf[b], preferred_element_type=F32) + jnp.dot(
            thl[1], abuf[8 + b], preferred_element_type=F32
        )
        return both[:COLS] + both[COLS:]

    def column_sum(term):
        acc = jnp.zeros((COLS, 128), F32)
        for b in range(8):
            acc = acc + fold(term(b))
        return total_of(acc)

    def arrived(rnd, direction):
        dots[...] = jnp.zeros_like(dots)

        def go(b):
            v = img[rnd, b]
            tokens_times(v, b)
            dots[...] += fold(v * direction(b))

        return go

    vacc[...] = jnp.zeros_like(vacc)
    sent0 = all_reduce(0, rhs_block, arrived(0, lambda b: img[0, b]))
    norm = total_of(dots[...])
    for h in range(2):
        t = products(h)
        set_tokens(h, t)
        tok[0, h] = t
        tok[1, h] = t
    vacc[...] = jnp.zeros_like(vacc)
    sent1 = all_reduce(1, image_block, arrived(1, lambda b: img[0, b]))
    alpha0 = norm / total_of(dots[...])
    for b in range(8):
        res[b] = img[0, b] - alpha0 * img[1, b]
    norm1 = column_sum(lambda b: res[b] * res[b])
    beta0 = norm1 / norm
    for h in range(2):
        t = tok[1, h] - alpha0 * products(h)
        tok[1, h] = t
        t = t + beta0 * tok[0, h]
        tok[0, h] = t
        set_tokens(h, t)

    def step_direction():
        for b in range(8):
            dir1[b] = res[b] + beta0 * img[0, b]

    vacc[...] = jnp.zeros_like(vacc)
    sent2 = all_reduce(2, image_block, arrived(2, lambda b: dir1[b]), step_direction)
    alpha1 = norm1 / total_of(dots[...])
    for b in range(8):
        res[b] = res[b] - alpha1 * img[2, b]
    norm2 = column_sum(lambda b: res[b] * res[b])
    beta = norm2 / norm1
    square = jnp.zeros((COLS, 128), F32)
    for h in range(2):
        t = tok[1, h] - alpha1 * products(h) + beta * tok[0, h]
        square = square + fold(t * t)
    diagonal = lax.broadcasted_iota(jnp.int32, (COLS, 128), 0) == lax.broadcasted_iota(jnp.int32, (COLS, 128), 1)
    curv[me] = jnp.sum(jnp.where(diagonal, total_of(square), 0.0), axis=0, keepdims=True)

    def kcopy(b):
        return remote(curv.at[me], curv.at[me], ks.at[b], kr.at[me], member(b))

    def krecv(b):
        return remote(curv.at[b], curv.at[b], ks.at[b], kr.at[b], member(b))

    @pl.loop(1, 8)
    def _(j):
        kcopy(lax.rem(me + j, 8)).start()

    known = alpha0 * img[0, me] + alpha1 * dir1[me]
    last = res[me] + beta * dir1[me]

    @pl.loop(1, 8)
    def _(j):
        krecv(lax.rem(me + j, 8)).wait_recv()

    curvature = curv[0]
    for b in range(1, 8):
        curvature = curvature + curv[b]
    alpha2 = norm2 / total_of(jnp.where(diagonal, curvature, 0.0))
    merged = known + alpha2 * last

    origin = lax.rem(zl + 4, 8)
    to_y, to_z, to_k = lax.div(origin, 2), 8 * lax.rem(origin, 2) + me, lax.div(x, 2)
    from_y, from_k = lax.div(zl, 2), lax.rem(zl, 2)
    slot = 2 * lax.rem(x, 2) + zh

    def out_self(dx):
        return (dx == x) & (to_y == y) & (to_z == z) & (to_k == k)

    def ocopy(dx):
        return remote(mblk.at[dx], obuf.at[slot], os.at[dx], orr.at[slot], dev(dx, to_y, to_z, to_k))

    for dx in range(4):
        mblk[dx] = merged[:, 128 * dx : 128 * (dx + 1)]

        @pl.when(jnp.logical_not(out_self(dx)))
        def _():
            ocopy(dx).start()

        @pl.when(out_self(dx))
        def _():
            obuf[slot] = mblk[dx]

    gather_sent()
    for sent in (sent0, sent1, sent2):
        sent()

    @pl.loop(1, 8)
    def _(j):
        kcopy(lax.rem(me + j, 8)).wait_send()

    for i in range(2):
        for h in range(2):
            q = 2 * i + h
            sx, sz = 2 * k + i, 8 * h + lax.rem(2 * y + zh + 4, 8)
            mine = (sx == x) & (from_y == y) & (sz == z) & (from_k == k)

            @pl.when(jnp.logical_not(mine))
            def _():
                remote(mblk.at[0], obuf.at[q], os.at[0], orr.at[q], dev(sx, from_y, sz, from_k)).wait_recv()

    for dx in range(4):

        @pl.when(jnp.logical_not(out_self(dx)))
        def _():
            ocopy(dx).wait_send()

    for q in range(4):
        out_ref[:, COLS * q : COLS * (q + 1)] = obuf[q].T


def local(activations, weights):
    dma = pltpu.SemaphoreType.DMA
    vmem = pltpu.VMEM
    return pl.pallas_call(
        kernel,
        out_shape=jax.ShapeDtypeStruct((128, 128), F32),
        in_specs=[pl.BlockSpec(memory_space=pl.ANY)] * 2,
        out_specs=pl.BlockSpec(memory_space=pltpu.VMEM),
        scratch_shapes=[
            vmem((16, 512, 512), BF16),
            vmem((2 * COLS, 4096), BF16),
            vmem((2 * COLS, 512), F32),
            vmem((2 * COLS, 512), BF16),
            vmem((2, COLS, 512), BF16),
            vmem((2, 2 * COLS, 512), BF16),
            vmem((3, 8, COLS, 512), F32),
            vmem((3, 4, COLS, 512), F32),
            vmem((3, 4, COLS, 512), F32),
            vmem((3, 8, COLS, 512), F32),
            vmem((8, COLS, 512), F32),
            vmem((8, COLS, 512), F32),
            vmem((2, 2 * COLS, 512), F32),
            vmem((2, 2, COLS, 512), F32),
            vmem((COLS, 128), F32),
            vmem((8, 1, 128), F32),
            vmem((4, COLS, 128), F32),
            vmem((4, COLS, 128), F32),
            vmem((8, COLS, 512), BF16),
            vmem((4, COLS, 512), BF16),
            vmem((8, COLS, 512), BF16),
            dma((2,)),
            dma((2, NP + 1, 8)),
            dma((2, NP + 1, 8)),
            dma((2, 16)),
            dma((2, 16)),
            dma((2, 16)),
            dma((2, 16)),
            dma((3,)),
            dma((3,)),
            dma((2,)),
            dma((2,)),
            dma((3, 4)),
            dma((3, 4)),
            dma((3, 4, CUTS)),
            dma((3, 4, CUTS)),
            dma((3, 4, CUTS)),
            dma((3, 4, CUTS)),
            dma((3, 4)),
            dma((3, 4)),
            dma((8,)),
            dma((8,)),
            dma((4,)),
            dma((4,)),
        ],
        compiler_params=pltpu.CompilerParams(
            collective_id=0, has_side_effects=True, vmem_limit_bytes=53 * 1024 * 1024 + 512 * 1024
        ),
    )(activations, jnp.swapaxes(weights, 1, 2))


def solution(mesh):
    in_specs = (P("mp", None, "row"), P("mp", None, ("row", "col")))
    out_specs = P(("row", "col"), "mp")
    return jax.shard_map(local, mesh=mesh, in_specs=in_specs, out_specs=out_specs, check_vma=False)
```

```python
import jax
import jax.numpy as jnp
from jax import lax
from jax.experimental import pallas as pl
from jax.experimental.pallas import tpu as pltpu
from jax.sharding import PartitionSpec as P

MESH = pl.DeviceIdType.MESH
F32 = jnp.float32
BF16 = jnp.bfloat16
NZ = (80, 80)
NP = len(NZ)
ZS = sum(NZ)
HALF = 176
COLS = 32
CUTS = 2


def fold(v):
    return v[:, :128] + v[:, 128:256] + v[:, 256:384] + v[:, 384:]


def total_of(v):
    return jnp.sum(v, axis=1, keepdims=True)


def kernel(
    a_hbm, w_hbm, out_ref,
    abuf, wbuf, yacc, yown, ycat, thl, ubuf, cbuf, rbuf, img, res, dir1, vacc, tok, dots, curv, mblk, obuf, narrow_parts, narrow_theirs, narrow_whole,
    in_sem, zs, zr, xs, xr, fs, fr, es, er, ys, yr, cs, cr, us, ur, gs, gr, hs, hr, ks, kr, os, orr,
):
    mp = lax.axis_index("mp")
    zl = lax.axis_index("row")
    x = lax.axis_index("col")
    y = lax.div(mp, 4)
    zh = lax.rem(lax.div(mp, 2), 2)
    k = lax.rem(mp, 2)
    z = 8 * zh + zl
    me = 2 * y + k

    def dev(dx, dy, dz, dk):
        return (4 * dy + 2 * lax.div(dz, 8) + dk, lax.rem(dz, 8), dx)

    def remote(src, dst, send, recv, device):
        return pltpu.make_async_remote_copy(
            src_ref=src, dst_ref=dst, send_sem=send, recv_sem=recv, device_id=device, device_id_type=MESH
        )

    def at_z(d):
        return lax.rem(z + d + 16, 16)

    def at_x(d):
        return lax.rem(x + d + 4, 4)

    def at_y(d):
        return lax.rem(y + d, 4)

    def member(b):
        return (4 * lax.div(b, 2) + 2 * zh + lax.rem(b, 2), zl, x)

    in_a = pltpu.make_async_copy(a_hbm.at[0], abuf.at[z], in_sem.at[0])
    in_w = pltpu.make_async_copy(w_hbm.at[0], wbuf, in_sem.at[1])
    in_a.start()
    in_w.start()

    barrier = pltpu.get_barrier_semaphore()

    def greet(device):
        pl.semaphore_signal(barrier, inc=1, device_id=device, device_id_type=MESH)

    greet(dev(x, y, at_z(1), k))
    greet(dev(x, y, at_z(-1), k))
    greet(dev(at_x(1), y, z, k))
    greet(dev(at_x(-1), y, z, k))

    @pl.loop(1, 8)
    def _(j):
        greet(member(lax.rem(me + j, 8)))

    in_a.wait()
    pl.semaphore_wait(barrier, 11)

    def piece(b, part, shard):
        if part < NP:
            return abuf.at[b, pl.ds(sum(NZ[:part]), NZ[part])]
        return abuf.at[b, pl.ds(ZS, 512 - ZS), pl.ds(pl.multiple_of(128 * shard, 128), 128)]

    def half_piece(b, d, shard):
        rows = pl.ds(ZS, HALF) if d == 0 else pl.ds(ZS + HALF, 512 - ZS - HALF)
        return abuf.at[b, rows, pl.ds(pl.multiple_of(128 * shard, 128), 128)]

    def steps(d, part):
        return 8 if (part < NP) == (d == 0) else 7

    def zlink(d, part, s, distance):
        sign = 1 - 2 * d
        ref = piece(at_z(-sign * distance), part, x)
        return remote(ref, ref, zs.at[d, part, s], zr.at[d, part, s], dev(x, y, at_z(sign), k))

    def zcopy(d, part, s):
        return zlink(d, part, s, s)

    def zrecv(d, part, s):
        return zlink(d, part, s, s + 1)

    def xcopy(d, b):
        ref = piece(b, NP, x)
        return remote(ref, ref, xs.at[d, b], xr.at[d, b], dev(at_x(1 - 2 * d), y, z, k))

    def xrecv(d, b):
        ref = piece(b, NP, at_x(2 * d - 1))
        return remote(ref, ref, xs.at[d, b], xr.at[d, b], dev(at_x(1 - 2 * d), y, z, k))

    def fcopy(d, b):
        ref = half_piece(b, d, at_x(2 * d - 1))
        return remote(ref, ref, fs.at[d, b], fr.at[d, b], dev(at_x(1 - 2 * d), y, z, k))

    def frecv(d, b):
        ref = half_piece(b, d, at_x(2))
        return remote(ref, ref, fs.at[d, b], fr.at[d, b], dev(at_x(1 - 2 * d), y, z, k))

    def finish(i, b):
        ref = piece(b, NP, at_x((1, -1, 2)[i]))
        return remote(ref, ref, es.at[i], er.at[i], dev(x, y, at_z(1 if i == 0 else -1), k))

    def pass_on(b):
        for d in range(2):
            xrecv(d, b).wait_recv()
            fcopy(d, b).start()

    def project(b):
        w = wbuf[:, pl.ds(pl.multiple_of(512 * lax.rem(b, 8), 512), 512)]
        yacc[...] += lax.dot_general(w, abuf[b], (((1,), (1,)), ((), ())), preferred_element_type=F32)

    def settle(b):
        for d in range(2):
            frecv(d, b).wait_recv()

        @pl.when(lax.div(b, 8) == zh)
        def _():
            project(b)

    for part in (NP, *range(NP)):
        for d in range(2):
            zcopy(d, part, 0).start()
    in_w.wait()
    yacc[...] = jnp.zeros_like(yacc)
    project(z)

    @pl.loop(1, 8)
    def _(s):
        def forward(part):
            for d in range(2):
                zrecv(d, part, s - 1).wait_recv()
                if steps(d, part) == 8:
                    zcopy(d, part, s).start()
                else:

                    @pl.when(s <= 6)
                    def _():
                        zcopy(d, part, s).start()

                if part == NP:
                    for e in range(2):
                        xcopy(e, at_z((2 * d - 1) * s)).start()

        forward(NP)

        @pl.when(s >= 2)
        def _():
            pass_on(at_z(1 - s))
            pass_on(at_z(s - 1))

        for part in range(NP):
            forward(part)

        @pl.when(s >= 3)
        def _():
            settle(at_z(2 - s))
            settle(at_z(s - 2))

    pass_on(at_z(7))
    finish(1, at_z(7)).start()
    pass_on(at_z(-7))
    finish(0, at_z(-7)).start()
    for d in (6, -6, 7, -7):
        settle(at_z(d))

    yown[...] = yacc[...].astype(BF16)

    def ycopy(i):
        to = at_z(4 - 8 * i)
        away = yown.at[pl.ds(pl.multiple_of(COLS * lax.div(to, 8), COLS), COLS)]
        return remote(away, ycat.at[zh], ys.at[i], yr.at[i], dev(x, y, to, k))

    def yrecv(i):
        h = lax.div(at_z(8 * i - 4), 8)
        return remote(yown.at[pl.ds(0, COLS)], ycat.at[h], ys.at[i], yr.at[i], dev(x, y, at_z(4 - 8 * i), k))

    ycopy(0).start()
    ycopy(1).start()
    finish(2, at_z(7)).start()

    for part in range(NP):
        zrecv(0, part, 7).wait_recv()
    zrecv(1, NP, 7).wait_recv()
    for i in range(3):
        finish(i, at_z(8)).wait_recv()

    def gather_sent():
        for i in range(3):
            finish(i, at_z(-7 if i == 0 else 7)).wait_send()
        for i in range(2):
            ycopy(i).wait_send()

        @pl.loop(1, 8)
        def _(j):
            for d in range(2):
                for b in (at_z(j), at_z(-j)):
                    xcopy(d, b).wait_send()
                    fcopy(d, b).wait_send()

        for d in range(2):
            for part in range(NP + 1):

                @pl.loop(0, steps(d, part))
                def _(s):
                    zcopy(d, part, s).wait_send()

    for i in range(2):
        yrecv(i).wait_recv()

    sibling = dev(x, y, z, 1 - k)

    def all_reduce(rnd, block, arrive, meanwhile=None):
        narrow = rnd == 2
        cuts = 1 if narrow else CUTS
        mine = ubuf.at[rnd]
        parts = narrow_parts if narrow else mine
        theirs = narrow_theirs if narrow else rbuf.at[rnd]
        whole = narrow_whole if narrow else img.at[rnd]

        def core_part(o):
            q = at_y(o)
            return remote(mine.at[2 * q + 1 - k], cbuf.at[rnd, q], cs.at[rnd, q], cr.at[rnd, q], sibling)

        def cut(c):
            return pl.ds(c * (COLS // cuts), COLS // cuts)

        def ring_part(o, c):
            q = at_y(o)
            src, dst = parts.at[2 * q + k, cut(c)], theirs.at[y, cut(c)]
            return remote(src, dst, us.at[rnd, q, c], ur.at[rnd, y, c], dev(x, q, z, k))

        def ring_part_from(o, c):
            q = at_y(o)
            src, dst = parts.at[2 * q + k, cut(c)], theirs.at[q, cut(c)]
            return remote(src, dst, us.at[rnd, q, c], ur.at[rnd, q, c], dev(x, q, z, k))

        def ring_whole(o, c):
            q = at_y(o)
            ref = whole.at[me, cut(c)]
            return remote(ref, ref, gs.at[rnd, q, c], gr.at[rnd, y, c], dev(x, q, z, k))

        def ring_whole_from(o, c):
            q = at_y(o)
            ref = whole.at[2 * q + k, cut(c)]
            return remote(ref, ref, gs.at[rnd, q, c], gr.at[rnd, q, c], dev(x, q, z, k))

        def core_whole(o):
            q = at_y(o)
            ref = whole.at[2 * q + k]
            return remote(ref, ref, hs.at[rnd, q], hr.at[rnd, q], sibling)

        def core_whole_from(o):
            q = at_y(o)
            ref = whole.at[2 * q + 1 - k]
            return remote(ref, ref, hs.at[rnd, q], hr.at[rnd, q], sibling)

        def give(o):
            b = 2 * at_y(o) + 1 - k
            mine[b] = block(b)
            core_part(o).start()

        def keep(o):
            q = at_y(o)
            b = 2 * q + k
            own = block(b)
            remote(mine.at[b], cbuf.at[rnd, q], cs.at[rnd, q], cr.at[rnd, q], sibling).wait_recv()
            if o:
                parts[b] = (own + cbuf[rnd, q]).astype(parts.dtype)
                ring_part(o, 0).start()
            else:
                img[rnd, me] = own + cbuf[rnd, q]

        def widened(b):
            if narrow:
                img[rnd, b] = whole[b].astype(F32)
            arrive(b)

        give(2)
        give(1)
        keep(2)
        give(3)
        keep(1)
        give(0)
        keep(3)
        for c in range(1, cuts):
            for o in (2, 1, 3):
                ring_part(o, c).start()
        keep(0)
        if meanwhile:
            meanwhile()
        for c in range(cuts):
            for o in (1, 3, 2):
                ring_part_from(o, c).wait_recv()
            total = img[rnd, me, cut(c)] + (
                theirs[at_y(1), cut(c)].astype(F32)
                + theirs[at_y(3), cut(c)].astype(F32)
                + theirs[at_y(2), cut(c)].astype(F32)
            )
            whole[me, cut(c)] = total.astype(whole.dtype)
            for o in (2, 1, 3):
                ring_whole(o, c).start()
        core_whole(0).start()
        widened(me)
        core_whole_from(0).wait_recv()
        widened(2 * y + 1 - k)
        for o in (1, 3, 2):
            for c in range(cuts):
                ring_whole_from(o, c).wait_recv()
            core_whole(o).start()
            widened(2 * at_y(o) + k)
        for o in (1, 3, 2):
            core_whole_from(o).wait_recv()
            widened(2 * at_y(o) + 1 - k)

        def sent():
            for o in range(4):
                core_part(o).wait_send()
                core_whole(o).wait_send()
                if o:
                    for c in range(cuts):
                        ring_part(o, c).wait_send()
                        ring_whole(o, c).wait_send()

        return sent

    def split(v):
        hi = v.astype(BF16)
        return hi, (v - hi.astype(F32)).astype(BF16)

    def tokens_times(v, b):
        both = jnp.concatenate(split(v), axis=0)
        for h in range(2):
            vacc[h] += lax.dot_general(
                both, abuf[8 * h + b], (((1,), (1,)), ((), ())), preferred_element_type=F32
            )

    def products(h):
        return vacc[h, :COLS] + vacc[h, COLS:]

    def set_tokens(h, v):
        hi, lo = split(v)
        thl[h, pl.ds(0, COLS)] = hi
        thl[h, pl.ds(COLS, COLS)] = lo

    def rhs_block(b):
        return jnp.dot(ycat[0], abuf[b], preferred_element_type=F32) + jnp.dot(
            ycat[1], abuf[8 + b], preferred_element_type=F32
        )

    def image_block(b):
        both = jnp.dot(thl[0], abuf[b], preferred_element_type=F32) + jnp.dot(
            thl[1], abuf[8 + b], preferred_element_type=F32
        )
        return both[:COLS] + both[COLS:]

    def column_sum(term):
        acc = jnp.zeros((COLS, 128), F32)
        for b in range(8):
            acc = acc + fold(term(b))
        return total_of(acc)

    def arrived(rnd, direction):
        dots[...] = jnp.zeros_like(dots)

        def go(b):
            v = img[rnd, b]
            tokens_times(v, b)
            dots[...] += fold(v * direction(b))

        return go

    vacc[...] = jnp.zeros_like(vacc)
    sent0 = all_reduce(0, rhs_block, arrived(0, lambda b: img[0, b]))
    norm = total_of(dots[...])
    for h in range(2):
        t = products(h)
        set_tokens(h, t)
        tok[0, h] = t
        tok[1, h] = t
    vacc[...] = jnp.zeros_like(vacc)
    sent1 = all_reduce(1, image_block, arrived(1, lambda b: img[0, b]))
    alpha0 = norm / total_of(dots[...])
    for b in range(8):
        res[b] = img[0, b] - alpha0 * img[1, b]
    norm1 = column_sum(lambda b: res[b] * res[b])
    beta0 = norm1 / norm
    for h in range(2):
        t = tok[1, h] - alpha0 * products(h)
        tok[1, h] = t
        t = t + beta0 * tok[0, h]
        tok[0, h] = t
        set_tokens(h, t)

    def step_direction():
        for b in range(8):
            dir1[b] = res[b] + beta0 * img[0, b]

    vacc[...] = jnp.zeros_like(vacc)
    sent2 = all_reduce(2, image_block, arrived(2, lambda b: dir1[b]), step_direction)
    alpha1 = norm1 / total_of(dots[...])
    for b in range(8):
        res[b] = res[b] - alpha1 * img[2, b]
    norm2 = column_sum(lambda b: res[b] * res[b])
    beta = norm2 / norm1
    square = jnp.zeros((COLS, 128), F32)
    for h in range(2):
        t = tok[1, h] - alpha1 * products(h) + beta * tok[0, h]
        square = square + fold(t * t)
    diagonal = lax.broadcasted_iota(jnp.int32, (COLS, 128), 0) == lax.broadcasted_iota(jnp.int32, (COLS, 128), 1)
    curv[me] = jnp.sum(jnp.where(diagonal, total_of(square), 0.0), axis=0, keepdims=True)

    def kcopy(b):
        return remote(curv.at[me], curv.at[me], ks.at[b], kr.at[me], member(b))

    def krecv(b):
        return remote(curv.at[b], curv.at[b], ks.at[b], kr.at[b], member(b))

    @pl.loop(1, 8)
    def _(j):
        kcopy(lax.rem(me + j, 8)).start()

    known = alpha0 * img[0, me] + alpha1 * dir1[me]
    last = res[me] + beta * dir1[me]

    @pl.loop(1, 8)
    def _(j):
        krecv(lax.rem(me + j, 8)).wait_recv()

    curvature = curv[0]
    for b in range(1, 8):
        curvature = curvature + curv[b]
    alpha2 = norm2 / total_of(jnp.where(diagonal, curvature, 0.0))
    merged = known + alpha2 * last

    origin = lax.rem(zl + 4, 8)
    to_y, to_z, to_k = lax.div(origin, 2), 8 * lax.rem(origin, 2) + me, lax.div(x, 2)
    from_y, from_k = lax.div(zl, 2), lax.rem(zl, 2)
    slot = 2 * lax.rem(x, 2) + zh

    def out_self(dx):
        return (dx == x) & (to_y == y) & (to_z == z) & (to_k == k)

    def ocopy(dx):
        return remote(mblk.at[dx], obuf.at[slot], os.at[dx], orr.at[slot], dev(dx, to_y, to_z, to_k))

    for dx in range(4):
        mblk[dx] = merged[:, 128 * dx : 128 * (dx + 1)]

        @pl.when(jnp.logical_not(out_self(dx)))
        def _():
            ocopy(dx).start()

        @pl.when(out_self(dx))
        def _():
            obuf[slot] = mblk[dx]

    gather_sent()
    for sent in (sent0, sent1, sent2):
        sent()

    @pl.loop(1, 8)
    def _(j):
        kcopy(lax.rem(me + j, 8)).wait_send()

    for i in range(2):
        for h in range(2):
            q = 2 * i + h
            sx, sz = 2 * k + i, 8 * h + lax.rem(2 * y + zh + 4, 8)
            mine = (sx == x) & (from_y == y) & (sz == z) & (from_k == k)

            @pl.when(jnp.logical_not(mine))
            def _():
                remote(mblk.at[0], obuf.at[q], os.at[0], orr.at[q], dev(sx, from_y, sz, from_k)).wait_recv()

    for dx in range(4):

        @pl.when(jnp.logical_not(out_self(dx)))
        def _():
            ocopy(dx).wait_send()

    for q in range(4):
        out_ref[:, COLS * q : COLS * (q + 1)] = obuf[q].T


def local(activations, weights):
    dma = pltpu.SemaphoreType.DMA
    vmem = pltpu.VMEM
    return pl.pallas_call(
        kernel,
        out_shape=jax.ShapeDtypeStruct((128, 128), F32),
        in_specs=[pl.BlockSpec(memory_space=pl.ANY)] * 2,
        out_specs=pl.BlockSpec(memory_space=pltpu.VMEM),
        scratch_shapes=[
            vmem((16, 512, 512), BF16),
            vmem((2 * COLS, 4096), BF16),
            vmem((2 * COLS, 512), F32),
            vmem((2 * COLS, 512), BF16),
            vmem((2, COLS, 512), BF16),
            vmem((2, 2 * COLS, 512), BF16),
            vmem((3, 8, COLS, 512), F32),
            vmem((3, 4, COLS, 512), F32),
            vmem((3, 4, COLS, 512), F32),
            vmem((3, 8, COLS, 512), F32),
            vmem((8, COLS, 512), F32),
            vmem((8, COLS, 512), F32),
            vmem((2, 2 * COLS, 512), F32),
            vmem((2, 2, COLS, 512), F32),
            vmem((COLS, 128), F32),
            vmem((8, 1, 128), F32),
            vmem((4, COLS, 128), F32),
            vmem((4, COLS, 128), F32),
            vmem((8, COLS, 512), BF16),
            vmem((4, COLS, 512), BF16),
            vmem((8, COLS, 512), BF16),
            dma((2,)),
            dma((2, NP + 1, 8)),
            dma((2, NP + 1, 8)),
            dma((2, 16)),
            dma((2, 16)),
            dma((2, 16)),
            dma((2, 16)),
            dma((3,)),
            dma((3,)),
            dma((2,)),
            dma((2,)),
            dma((3, 4)),
            dma((3, 4)),
            dma((3, 4, CUTS)),
            dma((3, 4, CUTS)),
            dma((3, 4, CUTS)),
            dma((3, 4, CUTS)),
            dma((3, 4)),
            dma((3, 4)),
            dma((8,)),
            dma((8,)),
            dma((4,)),
            dma((4,)),
        ],
        compiler_params=pltpu.CompilerParams(
            collective_id=0, has_side_effects=True, vmem_limit_bytes=53 * 1024 * 1024 + 512 * 1024
        ),
    )(activations, jnp.swapaxes(weights, 1, 2))


def solution(mesh):
    in_specs = (P("mp", None, "row"), P("mp", None, ("row", "col")))
    out_specs = P(("row", "col"), "mp")
    return jax.shard_map(local, mesh=mesh, in_specs=in_specs, out_specs=out_specs, check_vma=False)
```
